256 devices in a mesh: dp: 32 (over z, x), mp: 4 (over y), helper: 2 (over core).
Axes of the slice: x: 4, y: 4, z: 8, core: 2. Of those that a mesh axis runs over, the one named last changes fastest.
Arguments:
- activations: bfloat16 [4096, 2048], P('dp', ('mp', 'helper')), may hold values from -64 to 64
- output_grads: bfloat16 [4096, 16384], P('dp'), may hold values from -0.4375 to 0.4375
- left_state: float32 [4, 32, 512, 512], P('mp', 'dp', 'helper'), may hold values from -6 to 368640, as said below
- right_state: float32 [4, 32, 512, 512], P('mp', 'dp', 'helper'), may hold values from -6 to 122880, as said below
- left_root_old: bfloat16 [4, 32, 512, 512], P('mp', 'dp', 'helper'), may hold values from -0.00021 to 0.1205, as said below
- right_root_old: bfloat16 [4, 32, 512, 512], P('mp', 'dp'), may hold values from -0.00021 to 0.1205, as said below
- refresh: int32 [4, 32], P('mp', 'dp'), may hold values 0 or 1
Outputs:
- update: bfloat16 [4, 2, 256, 16384], P(None, 'helper', None, 'dp')
- left_new: float32 [4, 32, 512, 512], P('mp', 'dp', 'helper')
- right_new: float32 [4, 32, 512, 512], P('mp', 'dp', 'helper')
The draws below stay inside these ranges and needn't reach their ends.
Inputs may be any that keep to these rules, and one draw needn't show every extreme that they name: `left_state`: symmetric positive definite in each block. `right_state`: symmetric positive definite in each block. `left_root_old`: symmetric in each block. `right_root_old`: symmetric in each block.
All inputs are finite; a program needn't handle non-finite values. No bound on the sum of `refresh` on one device may be relied on, other than what follows from the above.
Results may differ from the reference program's by a relative error of at most 0.024.
Values may be sent and summed in bfloat16 or wider, within the bound.
A program may use at most 64 MiB of HBM per device.

```python
import math
import jax
import jax.numpy as jnp
from jax import lax

BLK = 512
ITERS = 2
TOK_DEV = 128
PIECE = 256
DIN = 2048
DOUT = 16384
TOKENS = 4096
N_DP = 32
N_MP = 4
N_HELPER = 2


def symmetric_noise(key, shape, spread):
    noise = jax.random.uniform(key, shape, jnp.float32, -spread, spread)
    return 0.5 * (noise + jnp.swapaxes(noise, -1, -2))


def place_diagonal(values, others):
    order = others.shape[-1]
    on_diagonal = jnp.arange(order)[:, None] == jnp.arange(order)[None, :]
    return jnp.where(on_diagonal, values[..., :, None], others)


def row_ramp(ratio):
    position = jnp.arange(BLK).astype(jnp.float32) / BLK
    return jnp.exp(position * math.log(ratio))


def draw_activations(key, part):
    key = jax.random.fold_in(key, 21)
    base_key, scale_key = jax.random.split(key, 2)
    position = (jnp.arange(DIN) % BLK).astype(jnp.float32)
    ramp = 1.0 + 2.0 * position / BLK
    column_scale = ramp * jnp.exp(jax.random.uniform(scale_key, (DIN,), jnp.float32, 0.0, math.log(3.5)))
    values = jnp.clip(jax.random.normal(base_key, (TOKENS, DIN), jnp.float32), -6.0, 6.0)
    return (values * column_scale[None, :]).astype(jnp.bfloat16)


def state_diagonal(key, base, ratio, spread):
    factor = jnp.exp(jax.random.uniform(key, (N_MP, N_DP, BLK), jnp.float32, 0.0, math.log(spread)))
    return base * row_ramp(ratio)[None, None, :] * factor


def draw_left_state(key, part):
    key = jax.random.fold_in(key, 11)
    noise_key, diagonal_key = jax.random.split(key)
    values = state_diagonal(diagonal_key, 8.0 * BLK, 30.0, 3.0)
    return place_diagonal(values, symmetric_noise(noise_key, (N_MP, N_DP, BLK, BLK), 6.0))


def draw_right_state(key, part):
    key = jax.random.fold_in(key, 12)
    noise_key, diagonal_key = jax.random.split(key)
    values = state_diagonal(diagonal_key, 8.0 * BLK, 10.0, 3.0)
    return place_diagonal(values, symmetric_noise(noise_key, (N_MP, N_DP, BLK, BLK), 6.0))


def draw_left_root_old(key, part):
    key = jax.random.fold_in(key, 13)
    noise_key, diagonal_key = jax.random.split(key)
    values = state_diagonal(diagonal_key, 0.06, 0.1, 2.0)
    return place_diagonal(values, symmetric_noise(noise_key, (N_MP, N_DP, BLK, BLK), 0.0002)).astype(jnp.bfloat16)


def draw_right_root_old(key, part):
    key = jax.random.fold_in(key, 14)
    noise_key, diagonal_key = jax.random.split(key)
    values = state_diagonal(diagonal_key, 0.06, 0.1, 2.0)
    return place_diagonal(values, symmetric_noise(noise_key, (N_MP, N_DP, BLK, BLK), 0.0002)).astype(jnp.bfloat16)


def plant(entries, own_key, low, top_value):
    longest = entries.shape.index(max(entries.shape))
    spots = []
    for shift in (0, 1):
        where = [jax.random.randint(jax.random.fold_in(own_key, axis), (), 0, length) for axis, length in enumerate(entries.shape)]
        where[longest] = (where[longest] + shift) % entries.shape[longest]
        spots.append(tuple(where))
    return entries.at[spots[0]].set(low).at[spots[1]].set(top_value)


def with_spikes(values, key, source, target, shards_of, factor):
    owner, partner = [(jnp.arange(values.shape[dim]) // (values.shape[dim] // shards_of)).reshape([-1 if axis == dim else 1 for axis in range(values.ndim)]) for dim in (source, target)]
    chosen = jax.random.permutation(key, shards_of)[partner]
    strong = (owner == chosen) | (owner == (partner + shards_of // 2) % shards_of)
    return jnp.where(strong, factor * values, values)


def block_levels(own_key, shape, cuts, least, largest):
    gain, own = 1.0, jax.random.fold_in(own_key, 6)
    for axis_at, blocks in cuts:
        heights = jnp.exp(jax.random.uniform(jax.random.fold_in(own, axis_at), (blocks,), jnp.float32, least / len(cuts), largest / len(cuts)))
        gain = gain * jnp.repeat(heights, shape[axis_at] // blocks).reshape([-1 if axis == axis_at else 1 for axis in range(len(shape))])
    return gain


def heavy_noise(key, dims, width, bound, pieces, heavy, kind=jnp.bfloat16):
    values = width * jax.random.normal(key, dims, jnp.float32)
    if pieces:
        values = values * block_levels(key, dims, pieces, -0.22, 0.18)
    return jnp.clip(with_spikes(values, jax.random.fold_in(key, 3), *heavy), -bound, bound).astype(kind)


def setup_inputs(seed: int = 0) -> dict:
    arg_keys = jax.random.split(jax.random.key(seed), 8)
    activations = draw_activations(jax.random.fold_in(arg_keys[7], 71), 0)
    output_grads = heavy_noise(arg_keys[1], (TOKENS, DOUT), (1.0 / TOKENS ** 0.5), 0.4375, ((0, 32),), (0, 1, 32, 2.75))
    left_state = draw_left_state(jax.random.fold_in(arg_keys[7], 71), 0)
    right_state = draw_right_state(jax.random.fold_in(arg_keys[7], 71), 0)
    left_root_old = draw_left_root_old(jax.random.fold_in(arg_keys[7], 71), 0)
    right_root_old = draw_right_root_old(jax.random.fold_in(arg_keys[7], 71), 0)
    refresh = plant((jax.random.randint(arg_keys[6], (N_MP, N_DP), 0, 2) < 1).astype(jnp.int32), jax.random.fold_in(arg_keys[6], 1), 0, 1)
    return dict(activations=activations, output_grads=output_grads, left_state=left_state, right_state=right_state, left_root_old=left_root_old, right_root_old=right_root_old, refresh=refresh)


decay_rate = 0.95
epsilon = 1e-06

def inverse_root(matrix):
    highest = lax.Precision.HIGHEST
    order = matrix.shape[0]
    identity = jnp.eye(order, dtype=matrix.dtype)
    scale = order * jnp.sqrt(jnp.mean(matrix * matrix) + epsilon)
    current = matrix / scale
    factor = (5.0 * identity - current) / 4.0
    result = factor * lax.rsqrt(jnp.sqrt(scale))
    for step in range(ITERS - 1):
        square = jnp.dot(factor, factor, precision=highest)
        quartic = jnp.dot(square, square, precision=highest)
        current = jnp.dot(quartic, current, precision=highest)
        factor = (5.0 * identity - current) / 4.0
        result = jnp.dot(result, factor, precision=highest)
    return result

def reference(activations, output_grads, left_state, right_state, left_root_old, right_root_old, refresh):
    highest = lax.Precision.HIGHEST
    shard_count = N_DP
    token_rows = activations.reshape(shard_count, TOK_DEV, DIN)
    grad_rows = output_grads.reshape(shard_count, TOK_DEV, DOUT)

    def add_shard(total, shard_pair):
        partial_sum = jnp.dot(shard_pair[0].T, shard_pair[1], preferred_element_type=jnp.float32)
        rounded = lax.optimization_barrier(partial_sum.astype(jnp.bfloat16))
        return (total + rounded.astype(jnp.float32), None)
    gradient, unused = lax.scan(add_shard, jnp.zeros((DIN, DOUT), jnp.float32), (token_rows, grad_rows))
    blocks = gradient.reshape(N_MP, BLK, N_DP, BLK).transpose(0, 2, 1, 3)
    left_new = decay_rate * left_state + jnp.einsum('ijab,ijcb->ijac', blocks, blocks, precision=highest)
    right_new = decay_rate * right_state + jnp.einsum('ijba,ijbc->ijac', blocks, blocks, precision=highest)
    count_blocks = N_MP * N_DP

    def flatten(array):
        return array.reshape((count_blocks,) + array.shape[2:])

    def roots_of(entry):
        left_fresh, right_fresh, left_stale, right_stale, flag = entry

        def renew():
            return (inverse_root(left_fresh).astype(jnp.bfloat16), inverse_root(right_fresh).astype(jnp.bfloat16))

        def keep_old():
            return (left_stale, right_stale)
        return lax.cond(flag > 0, renew, keep_old)
    left_root, right_root = lax.map(roots_of, (flatten(left_new), flatten(right_new), flatten(left_root_old), flatten(right_root_old), refresh.reshape(-1)))
    flat_grad = flatten(blocks)
    grad_half = flat_grad.astype(jnp.bfloat16)
    half_product = jnp.einsum('nab,nbc->nac', left_root.astype(jnp.float32), grad_half.astype(jnp.float32)).astype(jnp.bfloat16)
    shaped = jnp.einsum('nab,nbc->nac', half_product.astype(jnp.float32), right_root.astype(jnp.float32))
    graft_ratio = jnp.sqrt(lax.optimization_barrier(jnp.mean(flat_grad * flat_grad, axis=(1, 2))) + epsilon) / jnp.sqrt(lax.optimization_barrier(jnp.mean(shaped * shaped, axis=(1, 2))) + epsilon)
    scaled = (graft_ratio[:, None, None] * shaped).astype(jnp.bfloat16)
    update = scaled.reshape(N_MP, N_DP, N_HELPER, PIECE, BLK).transpose(0, 2, 3, 1, 4).reshape(N_MP, N_HELPER, PIECE, DOUT)
    return (update, left_new, right_new)
```

```python
import jax
import jax.numpy as jnp
from jax import lax
from jax.experimental import pallas as pl
from jax.experimental.pallas import tpu as pltpu
from jax.sharding import PartitionSpec as P

decay_rate = 0.95
epsilon = 1e-06

NZ, NX, NY = 8, 4, 4
BLK = 512
PIECE = 256
TOKENS = 128
ROWS = 16
ORDER = (0, 1, 7, 2, 6, 3, 5, 4)
SLOT = {distance: slot for slot, distance in enumerate(ORDER)}
STAGES = ((0, 0, 8), (1, 0, 8), (2, 0, 8), (3, 0, 4), (3, 4, 8))
VMEM_LIMIT = 56 * 2**20
MESH = pl.DeviceIdType.MESH


def place():
    d = lax.axis_index("dp")
    return d // NX, d % NX, lax.axis_index("mp"), lax.axis_index("helper")


def remote(src, dst, send, recv, device):
    return pltpu.make_async_remote_copy(
        src_ref=src,
        dst_ref=dst,
        send_sem=send,
        recv_sem=recv,
        device_id=device,
        device_id_type=MESH,
    )


def across_rows(a, b):
    return lax.dot_general(a, b, (((0,), (0,)), ((), ())), preferred_element_type=jnp.float32)


def inverse_root(s):
    b16 = jnp.bfloat16
    scale = BLK * jnp.sqrt(jnp.sum(s * s) * (1.0 / (BLK * BLK)) + epsilon)
    first = s * (1.0 / scale)
    first16 = first.astype(b16)
    second = jnp.dot(first16, first16, preferred_element_type=jnp.float32)
    third = jnp.dot(second.astype(b16), first16, preferred_element_type=jnp.float32)
    upper = (250.0 / 4096) * first - (25.0 / 4096) * second + (1.0 / 4096) * third
    high = jnp.dot(third.astype(b16), upper.astype(b16), preferred_element_type=jnp.float32)
    rows = lax.broadcasted_iota(jnp.int32, s.shape, 0)
    columns = lax.broadcasted_iota(jnp.int32, s.shape, 1)
    constant = jnp.where(rows == columns, 25.0 / 16, 0.0)
    low = (-5.0 / 16 - 3125.0 / 4096) * first + (3125.0 / 4096) * second - (1250.0 / 4096) * third
    return ((constant + low + high) * lax.rsqrt(jnp.sqrt(scale))).astype(b16)


def step_kernel(
    fresh,
    act_ref,
    og_ref,
    left_ref,
    right_ref,
    lroot_ref,
    rroot_ref,
    out,
    left_new,
    right_new,
    act_buf,
    act_t,
    act_other,
    act_t2,
    og_buf,
    q_buf,
    stats,
    lroot,
    rroot,
    piece,
    shaped,
    total,
    part_out,
    part_in,
    own_sem,
    z_send,
    z_recv,
    a_send,
    a_recv,
    x_send,
    x_recv,
    y_send,
    y_recv,
    c_send,
    c_recv,
    r_send,
    r_recv,
    s_send,
    s_recv,
    u_send,
    u_recv,
    out_sem,
):
    z, x, y, h = place()

    g = y * 2 + h

    pair = x + 1 - 2 * lax.rem(x, 2)
    partner = NX - 1 - x

    def at(dz, column=x):
        return (lax.rem(z + dz, NZ) * NX + column, y, h)

    def at_y(k):
        return (z * NX + x, lax.rem(y + k, NY), h)

    sibling = (z * NX + x, y, 1 - h)
    barrier = pltpu.get_barrier_semaphore()
    peers = [at(dz) for dz in range(1, NZ)] + [at(dz, pair) for dz in range(NZ)]
    peers += [at(0, partner), at_y(1), at_y(3), sibling]
    for peer in peers:
        pl.semaphore_signal(barrier, inc=1, device_id=peer, device_id_type=MESH)

    def start(copies):
        for copy in copies:
            copy.start()

    def await_bytes(ref, sem):
        pltpu.make_async_copy(ref, ref, sem).wait()

    here = pl.ds(pl.multiple_of(h * PIECE, PIECE), PIECE)
    there = pl.ds(pl.multiple_of((1 - h) * PIECE, PIECE), PIECE)

    def target(c):
        owner = pair if c % 2 else x
        return owner, (owner if c >= 2 else NX - 1 - owner)

    def og_part(dz, c):
        column = (lax.rem(z + dz, NZ) * NX + target(c)[1]) * BLK
        return og_ref.at[
            pl.ds(pl.multiple_of(g * ROWS, ROWS), ROWS), pl.ds(pl.multiple_of(column, BLK), BLK)
        ]

    own_og = [
        pltpu.make_async_copy(og_part(0, c), og_buf.at[c, 0, y, h], own_sem.at[c * 3])
        for c in (0, 2)
    ]
    own_act = pltpu.make_async_copy(act_ref, act_buf.at[0, 0], own_sem.at[1])
    start(own_og + [own_act])
    pl.semaphore_wait(barrier, len(peers))

    def send_og(i):
        c, first, end = STAGES[i]
        for slot in reversed(range(first, end)):
            if slot or c % 2:
                remote(
                    og_part(ORDER[slot], c),
                    og_buf.at[c, slot, y, h],
                    z_send.at[i],
                    z_recv.at[i],
                    at(ORDER[slot], target(c)[0]),
                ).start()

    def og_bytes(i):
        c, first, end = STAGES[i]
        return og_buf.at[c, first if c % 2 else first + 1 : end, 0, 0]

    def act_at(bank, distance, rows=slice(None)):
        return act_buf.at[bank, SLOT[distance % NZ], rows]

    def send_act(i):
        if i < 4:
            rows_up, rows_down = (slice(0, 2), slice(2, 4)) if i == 3 else (slice(None),) * 2
            up = act_at(0, i, rows_up) if i else act_ref
            down = act_at(0, -i, rows_down) if i else act_ref
            start(
                [
                    remote(up, act_at(0, i + 1, rows_up), a_send, a_recv.at[i], at(1)),
                    remote(down, act_at(0, -i - 1, rows_down), a_send, a_recv.at[i], at(7)),
                ]
            )
        for distance in (i, -i) if 0 < i < 4 else (i,):
            src = act_at(0, distance) if i else act_ref
            remote(src, act_at(1, distance), x_send, x_recv, at(0, pair)).start()

    def next_act(i):
        await_bytes(act_buf.at[0, 0:2] if i < 4 else act_buf.at[0, 0], a_recv.at[i - 1])
        send_act(i)

    low, high, far = lax.rem(y + 3, NY), lax.rem(y + 1, NY), lax.rem(y + 2, NY)

    def cross(i, rows):
        c, first, end = STAGES[i]
        if c < 3:
            ref = og_buf.at[c, first:end, rows, h]
            remote(ref, ref, c_send, c_recv.at[c], sibling).start()

    def first_y(i):
        c, first, end = STAGES[i]
        if c % 2 == 0:
            own_og[c // 2].wait()
        await_bytes(og_bytes(i), z_recv.at[i])
        mine = og_buf.at[c, first:end, y, h]
        start(
            [
                remote(mine, mine, y_send, y_recv.at[i, 0], at_y(1)),
                remote(mine, mine, y_send, y_recv.at[i, 0], at_y(3)),
            ]
        )
        cross(i, y)

    def second_y(i):
        c, first, end = STAGES[i]
        await_bytes(og_buf.at[c, first:end, 0:2, 0], y_recv.at[i, 0])
        middle = (first + end) // 2
        up, down = og_buf.at[c, first:middle, low, h], og_buf.at[c, middle:end, high, h]
        start(
            [
                remote(up, up, y_send, y_recv.at[i, 1], at_y(1)),
                remote(down, down, y_send, y_recv.at[i, 1], at_y(3)),
            ]
        )
        cross(i, low)
        cross(i, high)

    def third_y(i):
        c, first, end = STAGES[i]
        await_bytes(og_buf.at[c, first:end, 0, 0], y_recv.at[i, 1])
        cross(i, far)

    def turn(bank):
        act_t[bank] = act_buf[bank].reshape(NZ * TOKENS, PIECE).T

    def product(c):
        await_bytes(og_buf.at[c, :, :, 0], c_recv.at[c])
        rows = og_buf[c].reshape(NZ * TOKENS, BLK)
        part = jnp.dot(act_t[c % 2], rows, preferred_element_type=jnp.float32)
        if c == 1:
            part_out[...] = (total[...] + part).astype(jnp.bfloat16)
        else:
            total[...] = part

    def split_product(i):
        c, first, end = STAGES[i]
        rows = og_buf[c, first:end, :, h].reshape((end - first) * NY * ROWS, BLK)
        columns = act_t2[:, first * NY * ROWS : end * NY * ROWS]
        return jnp.dot(columns, rows, preferred_element_type=jnp.float32)

    olds = [
        pltpu.make_async_copy(left_ref, stats.at[0, here], own_sem.at[2]),
        pltpu.make_async_copy(right_ref, stats.at[1, here], own_sem.at[3]),
        pltpu.make_async_copy(lroot_ref, lroot.at[here], own_sem.at[4]),
        pltpu.make_async_copy(rroot_ref, rroot, own_sem.at[5]),
        remote(left_ref, stats.at[0, here], s_send.at[0], s_recv.at[0], sibling),
        remote(right_ref, stats.at[1, here], s_send.at[1], s_recv.at[1], sibling),
        remote(lroot_ref, lroot.at[here], s_send.at[2], s_recv.at[2], sibling),
    ]
    act_copy = remote(act_buf.at[1, :, :, 1 - h], act_other, s_send.at[4], s_recv.at[4], sibling)
    r_copy = remote(part_out, part_in, r_send, r_recv, at(0, partner))

    send_act(0)
    send_og(0)
    own_act.wait()
    for i in range(4):
        await_bytes(og_bytes(i), z_send.at[i])
        send_og(i + 1)
        next_act(i + 1)
        if i == 0:
            start(olds)
        first_y(i)
        if i >= 1:
            second_y(i - 1)
        if i >= 2:
            third_y(i - 2)
        if i == 3:
            turn(0)
            product(0)
    await_bytes(act_buf.at[1], x_recv)
    act_copy.start()
    first_y(4)
    second_y(3)
    third_y(2)
    turn(1)
    product(1)
    r_copy.start()
    second_y(4)
    third_y(3)
    product(2)
    for copy in olds:
        copy.wait()
    stats[...] = decay_rate * stats[...]
    act_copy.wait()
    act_t2[here] = act_buf[1, :, :, h].reshape(NZ * NY * ROWS, PIECE).T
    act_t2[there] = act_other[...].reshape(NZ * NY * ROWS, PIECE).T
    shaped[...] = split_product(3)
    r_copy.wait_recv()
    shaped[here] = shaped[here] + total[...] + part_in[...].astype(jnp.float32)
    third_y(4)
    shaped[...] = shaped[...] + split_product(4)
    q_buf[0] = shaped[...].astype(jnp.bfloat16)
    q_copy = remote(q_buf.at[0], q_buf.at[1], s_send.at[3], s_recv.at[3], sibling)
    q_copy.start()
    q_copy.wait_recv()
    grad_wide = q_buf[0].astype(jnp.float32) + q_buf[1].astype(jnp.float32)
    grad = grad_wide.astype(jnp.bfloat16)
    grad_square = jnp.sum(grad_wide * grad_wide)
    stats[1] = stats[1] + across_rows(grad, grad)
    right_copy = pltpu.make_async_copy(stats.at[1, here], right_new, out_sem.at[0])
    right_copy.start()
    stats[0] = stats[0] + lax.dot_general(
        grad, grad, (((1,), (1,)), ((), ())), preferred_element_type=jnp.float32
    )
    left_copy = pltpu.make_async_copy(stats.at[0, here], left_new, out_sem.at[1])
    left_copy.start()
    renew = fresh[0, 0] > 0
    lroot[...] = jnp.where(renew, inverse_root(stats[0]), lroot[...])
    rroot[...] = jnp.where(renew, inverse_root(stats[1]), rroot[...])
    half = jnp.dot(lroot[...], grad, preferred_element_type=jnp.float32).astype(jnp.bfloat16)
    shaped[...] = jnp.dot(half, rroot[...], preferred_element_type=jnp.float32)
    entries = 1.0 / (BLK * BLK)
    ratio = jnp.sqrt(grad_square * entries + epsilon) / jnp.sqrt(
        jnp.sum(shaped[...] * shaped[...]) * entries + epsilon
    )
    piece[...] = (ratio * shaped[here]).astype(jnp.bfloat16)

    below, above = lax.rem(y + 3, NY), lax.rem(y + 1, NY)
    bottom, top = pl.ds(0, PIECE // 2), pl.ds(PIECE // 2, PIECE // 2)

    def spread(i, rows, owner, k):
        src = piece.at[rows] if owner is y else out.at[owner, rows]
        return remote(src, out.at[owner, rows], u_send.at[i], u_recv.at[i], at_y(k))

    first = [spread(0, bottom, y, 1), spread(1, top, y, 3)]
    rest = [spread(2, top, y, 1), spread(3, bottom, y, 3)]
    second = [spread(4, bottom, below, 1), spread(5, top, above, 3)]
    start(first + rest)
    own_copy = pltpu.make_async_copy(piece, out.at[y], out_sem.at[2])
    own_copy.start()
    await_bytes(act_buf.at[0, 0 : NZ - 1], a_send)
    await_bytes(act_buf.at[0], x_send)
    await_bytes(og_buf.at[:, :, 0:3, 0], y_send)
    await_bytes(og_buf.at[0:3, :, :, 0], c_send)
    await_bytes(og_bytes(4), z_send.at[4])
    r_copy.wait_send()
    q_copy.wait_send()
    for one, two in zip(first, second):
        one.wait_recv()
        two.start()
    for copy in rest + second:
        copy.wait_recv()
    for copy in first + rest + second:
        copy.wait_send()
    for copy in (right_copy, left_copy, own_copy):
        copy.wait()


def step(fresh, act, og, left, right, lroot, rroot):
    hbm = pl.BlockSpec(memory_space=pl.ANY)
    dma = pltpu.SemaphoreType.DMA
    f32, b16 = jnp.float32, jnp.bfloat16
    return pl.pallas_call(
        step_kernel,
        out_shape=(
            pltpu.VMEM((NY, PIECE, BLK), b16),
            pltpu.VMEM((PIECE, BLK), f32),
            pltpu.VMEM((PIECE, BLK), f32),
        ),
        in_specs=[pl.BlockSpec(memory_space=pltpu.SMEM)] + [hbm] * 6,
        out_specs=(hbm,) * 3,
        scratch_shapes=[
            pltpu.VMEM((2, NZ, NY, 2, ROWS, PIECE), b16),
            pltpu.VMEM((2, PIECE, NZ * TOKENS), b16),
            pltpu.VMEM((NZ, NY, ROWS, PIECE), b16),
            pltpu.VMEM((BLK, NZ * NY * ROWS), b16),
            pltpu.VMEM((NX, NZ, NY, 2, ROWS, BLK), b16),
            pltpu.VMEM((2, BLK, BLK), b16),
            pltpu.VMEM((2, BLK, BLK), f32),
            pltpu.VMEM((BLK, BLK), b16),
            pltpu.VMEM((BLK, BLK), b16),
            pltpu.VMEM((PIECE, BLK), b16),
            pltpu.VMEM((BLK, BLK), f32),
            pltpu.VMEM((PIECE, BLK), f32),
            pltpu.VMEM((PIECE, BLK), b16),
            pltpu.VMEM((PIECE, BLK), b16),
            dma((7,)),
            dma((5,)),
            dma((5,)),
            dma,
            dma((4,)),
            dma,
            dma,
            dma,
            dma((5, 2)),
            dma,
            dma((3,)),
            dma,
            dma,
            dma((5,)),
            dma((5,)),
            dma((6,)),
            dma((6,)),
            dma((3,)),
        ],
        compiler_params=pltpu.CompilerParams(
            collective_id=0, has_side_effects=True, vmem_limit_bytes=VMEM_LIMIT
        ),
        name="step",
    )(fresh, act.reshape(NY, 2, ROWS, PIECE), og, left, right, lroot, rroot)


def finish_kernel(update, left, right, update_out, left_out, right_out, sems):
    copies = [
        pltpu.make_async_copy(update, update_out, sems.at[0]),
        pltpu.make_async_copy(left, left_out, sems.at[1]),
        pltpu.make_async_copy(right, right_out, sems.at[2]),
    ]
    for copy in copies:
        copy.start()
    for copy in copies:
        copy.wait()


def finish(*arrays):
    vmem = pl.BlockSpec(memory_space=pltpu.VMEM)
    anywhere = pl.BlockSpec(memory_space=pl.ANY)
    return pl.pallas_call(
        finish_kernel,
        out_shape=tuple(jax.ShapeDtypeStruct(a.shape, a.dtype) for a in arrays),
        in_specs=[vmem] * 3,
        out_specs=(anywhere,) * 3,
        scratch_shapes=[pltpu.SemaphoreType.DMA((3,))],
        compiler_params=pltpu.CompilerParams(vmem_limit_bytes=4 * 2**20),
        name="finish",
    )(*arrays)


def shards(act, og, left_state, right_state, left_root_old, right_root_old, refresh):
    update, left_new, right_new = finish(
        *step(
            refresh,
            act,
            og,
            left_state[0, 0],
            right_state[0, 0],
            left_root_old[0, 0],
            right_root_old[0, 0],
        )
    )
    return update[:, None], left_new[None, None], right_new[None, None]


def solution(mesh):
    placed = (
        P("dp", ("mp", "helper")),
        P("dp", None),
        P("mp", "dp", "helper", None),
        P("mp", "dp", "helper", None),
        P("mp", "dp", "helper", None),
        P("mp", "dp", None, None),
        P("mp", "dp"),
    )
    return jax.shard_map(
        shards,
        mesh=mesh,
        in_specs=placed,
        out_specs=(
            P(None, "helper", None, "dp"),
            P("mp", "dp", "helper", None),
            P("mp", "dp", "helper", None),
        ),
        check_vma=False,
    )
```

```python
import jax
import jax.numpy as jnp
from jax import lax
from jax.experimental import pallas as pl
from jax.experimental.pallas import tpu as pltpu
from jax.sharding import PartitionSpec as P

decay_rate = 0.95
epsilon = 1e-06

NZ, NX, NY = 8, 4, 4
BLK = 512
PIECE = 256
QUARTER = 64
TOKENS = 128
ROWS = 16
ORDER = (0, 1, 7, 2, 6, 3, 5, 4)
SLOT = {distance: slot for slot, distance in enumerate(ORDER)}
STAGES = ((0, 0, 8), (1, 0, 8), (2, 0, 8), (3, 0, 4), (3, 4, 8))
VMEM_LIMIT = 56 * 2**20
MESH = pl.DeviceIdType.MESH


def place():
    d = lax.axis_index("dp")
    return d // NX, d % NX, lax.axis_index("mp"), lax.axis_index("helper")


def remote(src, dst, send, recv, device):
    return pltpu.make_async_remote_copy(
        src_ref=src,
        dst_ref=dst,
        send_sem=send,
        recv_sem=recv,
        device_id=device,
        device_id_type=MESH,
    )


def across_rows(a, b):
    return lax.dot_general(a, b, (((0,), (0,)), ((), ())), preferred_element_type=jnp.float32)


def inverse_root(s):
    b16 = jnp.bfloat16
    scale = BLK * jnp.sqrt(jnp.sum(s * s) * (1.0 / (BLK * BLK)) + epsilon)
    first = s * (1.0 / scale)
    first16 = first.astype(b16)
    second = jnp.dot(first16, first16, preferred_element_type=jnp.float32)
    third = jnp.dot(second.astype(b16), first16, preferred_element_type=jnp.float32)
    upper = (250.0 / 4096) * first - (25.0 / 4096) * second + (1.0 / 4096) * third
    high = jnp.dot(third.astype(b16), upper.astype(b16), preferred_element_type=jnp.float32)
    rows = lax.broadcasted_iota(jnp.int32, s.shape, 0)
    columns = lax.broadcasted_iota(jnp.int32, s.shape, 1)
    constant = jnp.where(rows == columns, 25.0 / 16, 0.0)
    low = (-5.0 / 16 - 3125.0 / 4096) * first + (3125.0 / 4096) * second - (1250.0 / 4096) * third
    return ((constant + low + high) * lax.rsqrt(jnp.sqrt(scale))).astype(b16)


def step_kernel(
    fresh,
    act_ref,
    og_ref,
    left_ref,
    right_ref,
    lroot_ref,
    rroot_ref,
    out,
    left_new,
    right_new,
    act_buf,
    act_t,
    act_other,
    act_t2,
    og_buf,
    q_buf,
    stats,
    lroot,
    rroot,
    piece,
    shaped,
    total,
    part_out,
    part_in,
    own_sem,
    z_send,
    z_recv,
    a_send,
    a_recv,
    x_send,
    x_recv,
    y_send,
    y_recv,
    c_send,
    c_recv,
    r_send,
    r_recv,
    s_send,
    s_recv,
    u_send,
    u_recv,
    out_sem,
):
    z, x, y, h = place()

    g = y * 2 + h

    pair = x + 1 - 2 * lax.rem(x, 2)
    partner = NX - 1 - x

    def at(dz, column=x):
        return (lax.rem(z + dz, NZ) * NX + column, y, h)

    def at_y(k):
        return (z * NX + x, lax.rem(y + k, NY), h)

    sibling = (z * NX + x, y, 1 - h)
    barrier = pltpu.get_barrier_semaphore()
    peers = [at(dz) for dz in range(1, NZ)] + [at(dz, pair) for dz in range(NZ)]
    peers += [at(0, partner), at_y(1), at_y(3), sibling]
    for peer in peers:
        pl.semaphore_signal(barrier, inc=1, device_id=peer, device_id_type=MESH)

    def start(copies):
        for copy in copies:
            copy.start()

    def await_bytes(ref, sem):
        pltpu.make_async_copy(ref, ref, sem).wait()

    here = pl.ds(pl.multiple_of(h * PIECE, PIECE), PIECE)
    there = pl.ds(pl.multiple_of((1 - h) * PIECE, PIECE), PIECE)

    def target(c):
        owner = pair if c % 2 else x
        return owner, (owner if c >= 2 else NX - 1 - owner)

    def og_part(dz, c):
        column = (lax.rem(z + dz, NZ) * NX + target(c)[1]) * BLK
        return og_ref.at[
            pl.ds(pl.multiple_of(g * ROWS, ROWS), ROWS), pl.ds(pl.multiple_of(column, BLK), BLK)
        ]

    own_og = [
        pltpu.make_async_copy(og_part(0, c), og_buf.at[c, 0, y, h], own_sem.at[c * 3])
        for c in (0, 2)
    ]
    own_act = pltpu.make_async_copy(act_ref, act_buf.at[0, 0], own_sem.at[1])
    start(own_og + [own_act])
    pl.semaphore_wait(barrier, len(peers))

    def send_og(i):
        c, first, end = STAGES[i]
        for slot in reversed(range(first, end)):
            if slot or c % 2:
                remote(
                    og_part(ORDER[slot], c),
                    og_buf.at[c, slot, y, h],
                    z_send.at[i],
                    z_recv.at[i],
                    at(ORDER[slot], target(c)[0]),
                ).start()

    def og_bytes(i):
        c, first, end = STAGES[i]
        return og_buf.at[c, first if c % 2 else first + 1 : end, 0, 0]

    def act_at(bank, distance, rows=slice(None)):
        return act_buf.at[bank, SLOT[distance % NZ], rows]

    def send_act(i):
        if i < 4:
            rows_up, rows_down = (slice(0, 2), slice(2, 4)) if i == 3 else (slice(None),) * 2
            up = act_at(0, i, rows_up) if i else act_ref
            down = act_at(0, -i, rows_down) if i else act_ref
            start(
                [
                    remote(up, act_at(0, i + 1, rows_up), a_send, a_recv.at[i], at(1)),
                    remote(down, act_at(0, -i - 1, rows_down), a_send, a_recv.at[i], at(7)),
                ]
            )
        for distance in (i, -i) if 0 < i < 4 else (i,):
            src = act_at(0, distance) if i else act_ref
            remote(src, act_at(1, distance), x_send, x_recv, at(0, pair)).start()

    def next_act(i):
        await_bytes(act_buf.at[0, 0:2] if i < 4 else act_buf.at[0, 0], a_recv.at[i - 1])
        send_act(i)

    low, high, far = lax.rem(y + 3, NY), lax.rem(y + 1, NY), lax.rem(y + 2, NY)

    def cross(i, rows):
        c, first, end = STAGES[i]
        if c < 3:
            ref = og_buf.at[c, first:end, rows, h]
            remote(ref, ref, c_send, c_recv.at[c], sibling).start()

    def first_y(i):
        c, first, end = STAGES[i]
        if c % 2 == 0:
            own_og[c // 2].wait()
        await_bytes(og_bytes(i), z_recv.at[i])
        mine = og_buf.at[c, first:end, y, h]
        start(
            [
                remote(mine, mine, y_send, y_recv.at[i, 0], at_y(1)),
                remote(mine, mine, y_send, y_recv.at[i, 0], at_y(3)),
            ]
        )
        cross(i, y)

    def second_y(i):
        c, first, end = STAGES[i]
        await_bytes(og_buf.at[c, first:end, 0:2, 0], y_recv.at[i, 0])
        middle = (first + end) // 2
        up, down = og_buf.at[c, first:middle, low, h], og_buf.at[c, middle:end, high, h]
        start(
            [
                remote(up, up, y_send, y_recv.at[i, 1], at_y(1)),
                remote(down, down, y_send, y_recv.at[i, 1], at_y(3)),
            ]
        )
        cross(i, low)
        cross(i, high)

    def third_y(i):
        c, first, end = STAGES[i]
        await_bytes(og_buf.at[c, first:end, 0, 0], y_recv.at[i, 1])
        cross(i, far)

    def turn(bank):
        act_t[bank] = act_buf[bank].reshape(NZ * TOKENS, PIECE).T

    def product(c):
        await_bytes(og_buf.at[c, :, :, 0], c_recv.at[c])
        rows = og_buf[c].reshape(NZ * TOKENS, BLK)
        part = jnp.dot(act_t[c % 2], rows, preferred_element_type=jnp.float32)
        if c == 1:
            part_out[...] = (total[...] + part).astype(jnp.bfloat16)
        else:
            total[...] = part

    def split_product(i):
        c, first, end = STAGES[i]
        rows = og_buf[c, first:end, :, h].reshape((end - first) * NY * ROWS, BLK)
        columns = act_t2[:, first * NY * ROWS : end * NY * ROWS]
        return jnp.dot(columns, rows, preferred_element_type=jnp.float32)

    olds = [
        pltpu.make_async_copy(left_ref, stats.at[0, here], own_sem.at[2]),
        pltpu.make_async_copy(right_ref, stats.at[1, here], own_sem.at[3]),
        pltpu.make_async_copy(lroot_ref, lroot.at[here], own_sem.at[4]),
        pltpu.make_async_copy(rroot_ref, rroot, own_sem.at[5]),
        remote(left_ref, stats.at[0, here], s_send.at[0], s_recv.at[0], sibling),
        remote(right_ref, stats.at[1, here], s_send.at[1], s_recv.at[1], sibling),
        remote(lroot_ref, lroot.at[here], s_send.at[2], s_recv.at[2], sibling),
    ]
    act_copy = remote(act_buf.at[1, :, :, 1 - h], act_other, s_send.at[4], s_recv.at[4], sibling)
    r_copy = remote(part_out, part_in, r_send, r_recv, at(0, partner))

    send_act(0)
    send_og(0)
    send_og(1)
    own_act.wait()
    for i in range(4):
        await_bytes(og_bytes(i), z_send.at[i])
        if i < 3:
            send_og(i + 2)
        next_act(i + 1)
        if i == 0:
            start(olds)
        first_y(i)
        if i >= 1:
            second_y(i - 1)
        if i >= 2:
            third_y(i - 2)
        if i == 3:
            turn(0)
            product(0)
    await_bytes(act_buf.at[1], x_recv)
    act_copy.start()
    first_y(4)
    second_y(3)
    third_y(2)
    turn(1)
    product(1)
    r_copy.start()
    second_y(4)
    third_y(3)
    product(2)
    for copy in olds:
        copy.wait()
    stats[...] = decay_rate * stats[...]
    act_copy.wait()
    act_t2[here] = act_buf[1, :, :, h].reshape(NZ * NY * ROWS, PIECE).T
    act_t2[there] = act_other[...].reshape(NZ * NY * ROWS, PIECE).T
    shaped[...] = split_product(3)
    r_copy.wait_recv()
    shaped[here] = shaped[here] + total[...] + part_in[...].astype(jnp.float32)
    third_y(4)
    shaped[...] = shaped[...] + split_product(4)
    q_buf[0] = shaped[...].astype(jnp.bfloat16)
    q_copy = remote(q_buf.at[0], q_buf.at[1], s_send.at[3], s_recv.at[3], sibling)
    q_copy.start()
    q_copy.wait_recv()
    grad_wide = q_buf[0].astype(jnp.float32) + q_buf[1].astype(jnp.float32)
    grad = grad_wide.astype(jnp.bfloat16)
    grad_square = jnp.sum(grad_wide * grad_wide)
    stats[1] = stats[1] + across_rows(grad, grad)
    right_copy = pltpu.make_async_copy(stats.at[1, here], right_new, out_sem.at[0])
    right_copy.start()
    stats[0] = stats[0] + lax.dot_general(
        grad, grad, (((1,), (1,)), ((), ())), preferred_element_type=jnp.float32
    )
    left_copy = pltpu.make_async_copy(stats.at[0, here], left_new, out_sem.at[1])
    left_copy.start()
    renew = fresh[0, 0] > 0
    lroot[...] = jnp.where(renew, inverse_root(stats[0]), lroot[...])
    rroot[...] = jnp.where(renew, inverse_root(stats[1]), rroot[...])
    half = jnp.dot(lroot[...], grad, preferred_element_type=jnp.float32).astype(jnp.bfloat16)
    shaped[...] = jnp.dot(half, rroot[...], preferred_element_type=jnp.float32)
    entries = 1.0 / (BLK * BLK)
    ratio = jnp.sqrt(grad_square * entries + epsilon) / jnp.sqrt(
        jnp.sum(shaped[...] * shaped[...]) * entries + epsilon
    )
    piece[...] = (ratio * shaped[here]).astype(jnp.bfloat16)

    below, above = lax.rem(y + 3, NY), lax.rem(y + 1, NY)

    def spread(i, quarter, owner, k):
        rows = pl.ds(quarter * QUARTER, QUARTER)
        src = piece.at[rows] if owner is y else out.at[owner, rows]
        return remote(src, out.at[owner, rows], u_send.at[i], u_recv.at[i], at_y(k))

    up = [spread(q, q, y, 1) for q in range(4)]
    down = [spread(4 + q, 3 - q, y, 3) for q in range(4)]
    onward = [spread(8, 0, below, 1), spread(9, 3, above, 3)]
    onward += [spread(10, 1, below, 1), spread(11, 2, above, 3)]
    for one, two in zip(up, down):
        start([one, two])
    own_copy = pltpu.make_async_copy(piece, out.at[y], out_sem.at[2])
    own_copy.start()
    await_bytes(act_buf.at[0, 0 : NZ - 1], a_send)
    await_bytes(act_buf.at[0], x_send)
    await_bytes(og_buf.at[:, :, 0:3, 0], y_send)
    await_bytes(og_buf.at[0:3, :, :, 0], c_send)
    await_bytes(og_bytes(4), z_send.at[4])
    r_copy.wait_send()
    q_copy.wait_send()
    for one, two in zip((up[0], down[0], up[1], down[1]), onward):
        one.wait_recv()
        two.start()
    for copy in up[2:] + down[2:] + onward:
        copy.wait_recv()
    for copy in up + down + onward:
        copy.wait_send()
    for copy in (right_copy, left_copy, own_copy):
        copy.wait()


def step(fresh, act, og, left, right, lroot, rroot):
    hbm = pl.BlockSpec(memory_space=pl.ANY)
    dma = pltpu.SemaphoreType.DMA
    f32, b16 = jnp.float32, jnp.bfloat16
    return pl.pallas_call(
        step_kernel,
        out_shape=(
            pltpu.VMEM((NY, PIECE, BLK), b16),
            pltpu.VMEM((PIECE, BLK), f32),
            pltpu.VMEM((PIECE, BLK), f32),
        ),
        in_specs=[pl.BlockSpec(memory_space=pltpu.SMEM)] + [hbm] * 6,
        out_specs=(hbm,) * 3,
        scratch_shapes=[
            pltpu.VMEM((2, NZ, NY, 2, ROWS, PIECE), b16),
            pltpu.VMEM((2, PIECE, NZ * TOKENS), b16),
            pltpu.VMEM((NZ, NY, ROWS, PIECE), b16),
            pltpu.VMEM((BLK, NZ * NY * ROWS), b16),
            pltpu.VMEM((NX, NZ, NY, 2, ROWS, BLK), b16),
            pltpu.VMEM((2, BLK, BLK), b16),
            pltpu.VMEM((2, BLK, BLK), f32),
            pltpu.VMEM((BLK, BLK), b16),
            pltpu.VMEM((BLK, BLK), b16),
            pltpu.VMEM((PIECE, BLK), b16),
            pltpu.VMEM((BLK, BLK), f32),
            pltpu.VMEM((PIECE, BLK), f32),
            pltpu.VMEM((PIECE, BLK), b16),
            pltpu.VMEM((PIECE, BLK), b16),
            dma((7,)),
            dma((5,)),
            dma((5,)),
            dma,
            dma((4,)),
            dma,
            dma,
            dma,
            dma((5, 2)),
            dma,
            dma((3,)),
            dma,
            dma,
            dma((5,)),
            dma((5,)),
            dma((12,)),
            dma((12,)),
            dma((3,)),
        ],
        compiler_params=pltpu.CompilerParams(
            collective_id=0, has_side_effects=True, vmem_limit_bytes=VMEM_LIMIT
        ),
        name="step",
    )(fresh, act.reshape(NY, 2, ROWS, PIECE), og, left, right, lroot, rroot)


def finish_kernel(update, left, right, update_out, left_out, right_out, sems):
    copies = [
        pltpu.make_async_copy(update, update_out, sems.at[0]),
        pltpu.make_async_copy(left, left_out, sems.at[1]),
        pltpu.make_async_copy(right, right_out, sems.at[2]),
    ]
    for copy in copies:
        copy.start()
    for copy in copies:
        copy.wait()


def finish(*arrays):
    vmem = pl.BlockSpec(memory_space=pltpu.VMEM)
    anywhere = pl.BlockSpec(memory_space=pl.ANY)
    return pl.pallas_call(
        finish_kernel,
        out_shape=tuple(jax.ShapeDtypeStruct(a.shape, a.dtype) for a in arrays),
        in_specs=[vmem] * 3,
        out_specs=(anywhere,) * 3,
        scratch_shapes=[pltpu.SemaphoreType.DMA((3,))],
        compiler_params=pltpu.CompilerParams(vmem_limit_bytes=4 * 2**20),
        name="finish",
    )(*arrays)


def shards(act, og, left_state, right_state, left_root_old, right_root_old, refresh):
    update, left_new, right_new = finish(
        *step(
            refresh,
            act,
            og,
            left_state[0, 0],
            right_state[0, 0],
            left_root_old[0, 0],
            right_root_old[0, 0],
        )
    )
    return update[:, None], left_new[None, None], right_new[None, None]


def solution(mesh):
    placed = (
        P("dp", ("mp", "helper")),
        P("dp", None),
        P("mp", "dp", "helper", None),
        P("mp", "dp", "helper", None),
        P("mp", "dp", "helper", None),
        P("mp", "dp", None, None),
        P("mp", "dp"),
    )
    return jax.shard_map(
        shards,
        mesh=mesh,
        in_specs=placed,
        out_specs=(
            P(None, "helper", None, "dp"),
            P("mp", "dp", "helper", None),
            P("mp", "dp", "helper", None),
        ),
        check_vma=False,
    )
```

```python
import jax
import jax.numpy as jnp
from jax import lax
from jax.experimental import pallas as pl
from jax.experimental.pallas import tpu as pltpu
from jax.sharding import PartitionSpec as P

decay_rate = 0.95
epsilon = 1e-06

NZ, NX, NY = 8, 4, 4
BLK = 512
PIECE = 256
TOKENS = 128
ROWS = 32
ORDER = (0, 1, 7, 2, 6, 3, 5, 4)
SLOT = {distance: slot for slot, distance in enumerate(ORDER)}
STAGES = ((0, 0, 8), (1, 0, 8), (2, 0, 8), (3, 0, 4), (3, 4, 8))
VMEM_LIMIT = 56 * 2**20
MESH = pl.DeviceIdType.MESH


def place():
    d = lax.axis_index("dp")
    return d // NX, d % NX, lax.axis_index("mp"), lax.axis_index("helper")


def remote(src, dst, send, recv, device):
    return pltpu.make_async_remote_copy(
        src_ref=src,
        dst_ref=dst,
        send_sem=send,
        recv_sem=recv,
        device_id=device,
        device_id_type=MESH,
    )


def across_rows(a, b):
    return lax.dot_general(a, b, (((0,), (0,)), ((), ())), preferred_element_type=jnp.float32)


def inverse_root(s):
    b16 = jnp.bfloat16
    scale = BLK * jnp.sqrt(jnp.sum(s * s) * (1.0 / (BLK * BLK)) + epsilon)
    first = s * (1.0 / scale)
    first16 = first.astype(b16)
    second = jnp.dot(first16, first16, preferred_element_type=jnp.float32)
    third = jnp.dot(second.astype(b16), first16, preferred_element_type=jnp.float32)
    upper = (250.0 / 4096) * first - (25.0 / 4096) * second + (1.0 / 4096) * third
    high = jnp.dot(third.astype(b16), upper.astype(b16), preferred_element_type=jnp.float32)
    rows = lax.broadcasted_iota(jnp.int32, s.shape, 0)
    columns = lax.broadcasted_iota(jnp.int32, s.shape, 1)
    constant = jnp.where(rows == columns, 25.0 / 16, 0.0)
    low = (-5.0 / 16 - 3125.0 / 4096) * first + (3125.0 / 4096) * second - (1250.0 / 4096) * third
    return ((constant + low + high) * lax.rsqrt(jnp.sqrt(scale))).astype(b16)


def step_kernel(
    fresh,
    act_ref,
    og_ref,
    left_ref,
    right_ref,
    lroot_ref,
    rroot_ref,
    out,
    left_new,
    right_new,
    act_buf,
    act_t,
    og_buf,
    part_out,
    part_in,
    grad_buf,
    stats,
    lroot,
    rroot,
    piece,
    shaped,
    total,
    own_sem,
    z_send,
    z_recv,
    a_send,
    a_recv,
    x_send,
    x_recv,
    y_send,
    y_recv,
    r_send,
    r_recv,
    s_send,
    s_recv,
    u_send,
    u_recv,
    out_sem,
):
    z, x, y, h = place()

    pair = x + 1 - 2 * lax.rem(x, 2)
    partner = NX - 1 - x

    def at(dz, column=x):
        return (lax.rem(z + dz, NZ) * NX + column, y, h)

    def crossed(dz, column=x):
        return (lax.rem(z + dz, NZ) * NX + column, y, 1 - h)

    def at_y(k):
        return (z * NX + x, lax.rem(y + k, NY), h)

    sibling = crossed(0)
    barrier = pltpu.get_barrier_semaphore()
    peers = [crossed(dz) for dz in range(NZ)] + [crossed(dz, pair) for dz in range(NZ)]
    peers += [at(1), at(7), at(0, pair), at(0, partner), at_y(1), at_y(3)]
    for peer in peers:
        pl.semaphore_signal(barrier, inc=1, device_id=peer, device_id_type=MESH)

    def start(copies):
        for copy in copies:
            copy.start()

    def await_bytes(ref, sem):
        pltpu.make_async_copy(ref, ref, sem).wait()

    here = pl.ds(pl.multiple_of(h * PIECE, PIECE), PIECE)

    def target(c):
        owner = pair if c % 2 else x
        return owner, (owner if c >= 2 else NX - 1 - owner)

    def og_part(dz, c):
        column = (lax.rem(z + dz, NZ) * NX + target(c)[1]) * BLK
        return og_ref.at[
            pl.ds(pl.multiple_of(y * ROWS, ROWS), ROWS), pl.ds(pl.multiple_of(column, BLK), BLK)
        ]

    def old_copies():
        return [
            pltpu.make_async_copy(left_ref, stats.at[0, here], own_sem.at[2]),
            pltpu.make_async_copy(right_ref, stats.at[1, here], own_sem.at[3]),
            pltpu.make_async_copy(lroot_ref, lroot.at[here], own_sem.at[4]),
            pltpu.make_async_copy(rroot_ref, rroot, own_sem.at[5]),
            remote(left_ref, stats.at[0, here], s_send.at[0], s_recv.at[0], sibling),
            remote(right_ref, stats.at[1, here], s_send.at[1], s_recv.at[1], sibling),
            remote(lroot_ref, lroot.at[here], s_send.at[2], s_recv.at[2], sibling),
        ]

    def age():
        for copy in old_copies():
            copy.wait()
        stats[...] = decay_rate * stats[...]

    g_copy = remote(grad_buf, grad_buf, s_send.at[3], s_recv.at[3], sibling)
    pl.semaphore_wait(barrier, len(peers))

    @pl.when(h == 0)
    def _():
        start(
            [
                remote(act_ref, act_buf.at[0, SLOT[1], 0], a_send, a_recv.at[0], crossed(1)),
                remote(act_ref, act_buf.at[0, SLOT[7], 0], a_send, a_recv.at[0], crossed(7)),
                remote(act_ref, act_buf.at[0, 0, 0], a_send, a_recv.at[4], sibling),
            ]
        )
        for i, (c, first, end) in enumerate(STAGES):
            for slot in reversed(range(first, end)):
                if slot or c % 2:
                    remote(
                        og_part(ORDER[slot], c),
                        og_buf.at[c, slot, y],
                        z_send,
                        z_recv.at[i],
                        crossed(ORDER[slot], target(c)[0]),
                    ).start()
            if i == 0:
                remote(act_ref, act_buf.at[1, 0, 0], a_send, x_recv, crossed(0, pair)).start()
        start(old_copies())
        age()
        g_copy.wait_recv()

    @pl.when(h == 1)
    def _():
        own_og = [
            pltpu.make_async_copy(og_part(0, c), og_buf.at[c, 0, y], own_sem.at[c * 3])
            for c in (0, 2)
        ]
        own_act = pltpu.make_async_copy(act_ref, act_buf.at[0, 0, 1], own_sem.at[1])

        def send_act(i):
            up, down = act_buf.at[0, SLOT[i]], act_buf.at[0, SLOT[-i % NZ]]
            if i < 4:
                to_up, to_down = act_buf.at[0, SLOT[i + 1]], act_buf.at[0, SLOT[7 - i]]
                if i == 3:
                    up, to_up, down, to_down = up.at[0], to_up.at[0], down.at[1], to_down.at[1]
                if i == 0:
                    up, to_up, down, to_down = act_ref, to_up.at[1], act_ref, to_down.at[1]
                start(
                    [
                        remote(up, to_up, a_send, a_recv.at[i], at(1)),
                        remote(down, to_down, a_send, a_recv.at[i], at(7)),
                    ]
                )
            if i == 0:
                remote(act_ref, act_buf.at[1, 0, 1], x_send, x_recv, at(0, pair)).start()
                return
            for slot in (SLOT[i], SLOT[-i % NZ]) if i < 4 else (SLOT[i],):
                src, dst = act_buf.at[0, slot], act_buf.at[1, slot]
                remote(src, dst, x_send, x_recv, at(0, pair)).start()

        def next_act(i):
            await_bytes(act_buf.at[0, 0:2] if i < 4 else act_buf.at[0, 0], a_recv.at[i - 1])
            send_act(i)

        low, high = lax.rem(y + 3, NY), lax.rem(y + 1, NY)

        def first_y(i):
            c, first, end = STAGES[i]
            if c % 2 == 0:
                own_og[c // 2].wait()
            await_bytes(og_buf.at[c, first if c % 2 else first + 1 : end, 0], z_recv.at[i])
            mine = og_buf.at[c, first:end, y]
            start(
                [
                    remote(mine, mine, y_send, y_recv.at[i, 0], at_y(1)),
                    remote(mine, mine, y_send, y_recv.at[i, 0], at_y(3)),
                ]
            )

        def second_y(i):
            c, first, end = STAGES[i]
            await_bytes(og_buf.at[c, first:end, 0:2], y_recv.at[i, 0])
            middle = (first + end) // 2
            up, down = og_buf.at[c, first:middle, low], og_buf.at[c, middle:end, high]
            start(
                [
                    remote(up, up, y_send, y_recv.at[i, 1], at_y(1)),
                    remote(down, down, y_send, y_recv.at[i, 1], at_y(3)),
                ]
            )

        def turn(bank):
            for half in range(2):
                columns = act_buf[bank, :, half].reshape(NZ * TOKENS, PIECE)
                act_t[bank, pl.ds(half * PIECE, PIECE)] = columns.T

        def product(i):
            c, first, end = STAGES[i]
            await_bytes(og_buf.at[c, first:end, 0], y_recv.at[i, 1])
            rows = og_buf[c, first:end].reshape((end - first) * TOKENS, BLK)
            columns = act_t[c % 2, :, first * TOKENS : end * TOKENS]
            return jnp.dot(columns, rows, preferred_element_type=jnp.float32)

        start(own_og + [own_act])
        send_act(0)
        next_act(1)
        first_y(0)
        next_act(2)
        start(old_copies())
        first_y(1)
        second_y(0)
        next_act(3)
        first_y(2)
        second_y(1)
        own_act.wait()
        await_bytes(act_buf.at[0, 0, 0], a_recv.at[4])
        next_act(4)
        turn(0)
        total[...] = product(0)
        first_y(3)
        second_y(2)
        await_bytes(act_buf.at[1], x_recv)
        turn(1)
        part_out[...] = (total[...] + product(1)).astype(jnp.bfloat16)
        r_copy = remote(part_out, part_in, r_send, r_recv, at(0, partner))
        r_copy.start()
        first_y(4)
        second_y(3)
        total[...] = product(2)
        second_y(4)
        total[...] = total[...] + product(3)
        age()
        r_copy.wait_recv()
        total[...] = total[...] + part_in[...].astype(jnp.float32)
        grad_buf[...] = (total[...] + product(4)).astype(jnp.bfloat16)
        g_copy.start()

    grad = grad_buf[...]
    grad_wide = grad.astype(jnp.float32)
    grad_square = jnp.sum(grad_wide * grad_wide)
    stats[1] = stats[1] + across_rows(grad, grad)
    right_copy = pltpu.make_async_copy(stats.at[1, here], right_new, out_sem.at[0])
    right_copy.start()
    stats[0] = stats[0] + lax.dot_general(
        grad, grad, (((1,), (1,)), ((), ())), preferred_element_type=jnp.float32
    )
    left_copy = pltpu.make_async_copy(stats.at[0, here], left_new, out_sem.at[1])
    left_copy.start()
    renew = fresh[0, 0] > 0
    lroot[...] = jnp.where(renew, inverse_root(stats[0]), lroot[...])
    rroot[...] = jnp.where(renew, inverse_root(stats[1]), rroot[...])
    half = jnp.dot(lroot[...], grad, preferred_element_type=jnp.float32).astype(jnp.bfloat16)
    shaped[...] = jnp.dot(half, rroot[...], preferred_element_type=jnp.float32)
    entries = 1.0 / (BLK * BLK)
    ratio = jnp.sqrt(grad_square * entries + epsilon) / jnp.sqrt(
        jnp.sum(shaped[...] * shaped[...]) * entries + epsilon
    )
    piece[...] = (ratio * shaped[here]).astype(jnp.bfloat16)

    below, above = lax.rem(y + 3, NY), lax.rem(y + 1, NY)
    bottom, top = pl.ds(0, PIECE // 2), pl.ds(PIECE // 2, PIECE // 2)

    def spread(i, rows, owner, k):
        src = piece.at[rows] if owner is y else out.at[owner, rows]
        return remote(src, out.at[owner, rows], u_send.at[i], u_recv.at[i], at_y(k))

    first = [spread(0, bottom, y, 1), spread(1, top, y, 3)]
    rest = [spread(2, top, y, 1), spread(3, bottom, y, 3)]
    second = [spread(4, bottom, below, 1), spread(5, top, above, 3)]
    start(first + rest)
    own_copy = pltpu.make_async_copy(piece, out.at[y], out_sem.at[2])
    own_copy.start()

    @pl.when(h == 0)
    def _():
        await_bytes(act_buf.at[0, 0:2], a_send)
        await_bytes(og_buf.at[0:3, 0:5, 0:2], z_send)

    @pl.when(h == 1)
    def _():
        await_bytes(act_buf.at[0, 0:6], a_send)
        await_bytes(og_buf.at[0:3, 0:5, 0:2], x_send)
        await_bytes(og_buf.at[:, :, 0:3], y_send)
        await_bytes(part_out, r_send)
        g_copy.wait_send()

    for one, two in zip(first, second):
        one.wait_recv()
        two.start()
    for copy in rest + second:
        copy.wait_recv()
    for copy in first + rest + second:
        copy.wait_send()
    for copy in (right_copy, left_copy, own_copy):
        copy.wait()


def step(fresh, act, og, left, right, lroot, rroot):
    hbm = pl.BlockSpec(memory_space=pl.ANY)
    dma = pltpu.SemaphoreType.DMA
    f32, b16 = jnp.float32, jnp.bfloat16
    return pl.pallas_call(
        step_kernel,
        out_shape=(
            pltpu.VMEM((NY, PIECE, BLK), b16),
            pltpu.VMEM((PIECE, BLK), f32),
            pltpu.VMEM((PIECE, BLK), f32),
        ),
        in_specs=[pl.BlockSpec(memory_space=pltpu.SMEM)] + [hbm] * 6,
        out_specs=(hbm,) * 3,
        scratch_shapes=[
            pltpu.VMEM((2, NZ, 2, TOKENS, PIECE), b16),
            pltpu.VMEM((2, BLK, NZ * TOKENS), b16),
            pltpu.VMEM((4, NZ, NY, ROWS, BLK), b16),
            pltpu.VMEM((BLK, BLK), b16),
            pltpu.VMEM((BLK, BLK), b16),
            pltpu.VMEM((BLK, BLK), b16),
            pltpu.VMEM((2, BLK, BLK), f32),
            pltpu.VMEM((BLK, BLK), b16),
            pltpu.VMEM((BLK, BLK), b16),
            pltpu.VMEM((PIECE, BLK), b16),
            pltpu.VMEM((BLK, BLK), f32),
            pltpu.VMEM((BLK, BLK), f32),
            dma((7,)),
            dma,
            dma((5,)),
            dma,
            dma((5,)),
            dma,
            dma,
            dma,
            dma((5, 2)),
            dma,
            dma,
            dma((4,)),
            dma((4,)),
            dma((6,)),
            dma((6,)),
            dma((3,)),
        ],
        compiler_params=pltpu.CompilerParams(
            collective_id=0, has_side_effects=True, vmem_limit_bytes=VMEM_LIMIT
        ),
        name="step",
    )(fresh, act, og, left, right, lroot, rroot)


def finish_kernel(update, left, right, update_out, left_out, right_out, sems):
    copies = [
        pltpu.make_async_copy(update, update_out, sems.at[0]),
        pltpu.make_async_copy(left, left_out, sems.at[1]),
        pltpu.make_async_copy(right, right_out, sems.at[2]),
    ]
    for copy in copies:
        copy.start()
    for copy in copies:
        copy.wait()


def finish(*arrays):
    vmem = pl.BlockSpec(memory_space=pltpu.VMEM)
    anywhere = pl.BlockSpec(memory_space=pl.ANY)
    return pl.pallas_call(
        finish_kernel,
        out_shape=tuple(jax.ShapeDtypeStruct(a.shape, a.dtype) for a in arrays),
        in_specs=[vmem] * 3,
        out_specs=(anywhere,) * 3,
        scratch_shapes=[pltpu.SemaphoreType.DMA((3,))],
        compiler_params=pltpu.CompilerParams(vmem_limit_bytes=4 * 2**20),
        name="finish",
    )(*arrays)


def shards(act, og, left_state, right_state, left_root_old, right_root_old, refresh):
    update, left_new, right_new = finish(
        *step(
            refresh,
            act,
            og,
            left_state[0, 0],
            right_state[0, 0],
            left_root_old[0, 0],
            right_root_old[0, 0],
        )
    )
    return update[:, None], left_new[None, None], right_new[None, None]


def solution(mesh):
    placed = (
        P("dp", ("mp", "helper")),
        P("dp", None),
        P("mp", "dp", "helper", None),
        P("mp", "dp", "helper", None),
        P("mp", "dp", "helper", None),
        P("mp", "dp", None, None),
        P("mp", "dp"),
    )
    return jax.shard_map(
        shards,
        mesh=mesh,
        in_specs=placed,
        out_specs=(
            P(None, "helper", None, "dp"),
            P("mp", "dp", "helper", None),
            P("mp", "dp", "helper", None),
        ),
        check_vma=False,
    )
```

```python
import jax
import jax.numpy as jnp
from jax import lax
from jax.experimental import pallas as pl
from jax.experimental.pallas import tpu as pltpu
from jax.sharding import PartitionSpec as P

decay_rate = 0.95
epsilon = 1e-06

NZ, NX, NY = 8, 4, 4
BLK = 512
PIECE = 256
TOKENS = 128
ROWS = 32
ORDER = (0, 1, 7, 2, 6, 3, 5, 4)
SLOT = {distance: slot for slot, distance in enumerate(ORDER)}
STAGES = ((0, 0, 8), (1, 0, 8), (2, 0, 8), (3, 0, 4), (3, 4, 8))
VMEM_LIMIT = 56 * 2**20
MESH = pl.DeviceIdType.MESH


def place():
    d = lax.axis_index("dp")
    return d // NX, d % NX, lax.axis_index("mp"), lax.axis_index("helper")


def remote(src, dst, send, recv, device):
    return pltpu.make_async_remote_copy(
        src_ref=src,
        dst_ref=dst,
        send_sem=send,
        recv_sem=recv,
        device_id=device,
        device_id_type=MESH,
    )


def across_rows(a, b):
    return lax.dot_general(a, b, (((0,), (0,)), ((), ())), preferred_element_type=jnp.float32)


def inverse_root(s):
    b16 = jnp.bfloat16
    scale = BLK * jnp.sqrt(jnp.sum(s * s) * (1.0 / (BLK * BLK)) + epsilon)
    first = s * (1.0 / scale)
    first16 = first.astype(b16)
    second = jnp.dot(first16, first16, preferred_element_type=jnp.float32)
    third = jnp.dot(second.astype(b16), first16, preferred_element_type=jnp.float32)
    upper = (250.0 / 4096) * first - (25.0 / 4096) * second + (1.0 / 4096) * third
    high = jnp.dot(third.astype(b16), upper.astype(b16), preferred_element_type=jnp.float32)
    rows = lax.broadcasted_iota(jnp.int32, s.shape, 0)
    columns = lax.broadcasted_iota(jnp.int32, s.shape, 1)
    constant = jnp.where(rows == columns, 25.0 / 16, 0.0)
    low = (-5.0 / 16 - 3125.0 / 4096) * first + (3125.0 / 4096) * second - (1250.0 / 4096) * third
    return ((constant + low + high) * lax.rsqrt(jnp.sqrt(scale))).astype(b16)


def step_kernel(
    fresh,
    act_ref,
    og_ref,
    left_ref,
    right_ref,
    lroot_ref,
    rroot_ref,
    out,
    left_new,
    right_new,
    act_raw,
    act_own,
    act_buf,
    og_buf,
    part_out,
    part_in,
    grad_buf,
    stats,
    lroot,
    rroot,
    piece,
    shaped,
    total,
    own_sem,
    z_send,
    z_recv,
    a_send,
    a_recv,
    x_send,
    x_recv,
    y_send,
    y_recv,
    r_send,
    r_recv,
    s_send,
    s_recv,
    u_send,
    u_recv,
    out_sem,
):
    z, x, y, h = place()

    pair = x + 1 - 2 * lax.rem(x, 2)
    partner = NX - 1 - x

    def at(dz, column=x):
        return (lax.rem(z + dz, NZ) * NX + column, y, h)

    def crossed(dz, column=x):
        return (lax.rem(z + dz, NZ) * NX + column, y, 1 - h)

    def at_y(k):
        return (z * NX + x, lax.rem(y + k, NY), h)

    sibling = crossed(0)
    barrier = pltpu.get_barrier_semaphore()
    peers = [crossed(dz) for dz in range(NZ)] + [crossed(dz, pair) for dz in range(NZ)]
    peers += [at(1), at(7), at(0, pair), at(0, partner), at_y(1), at_y(3)]
    for peer in peers:
        pl.semaphore_signal(barrier, inc=1, device_id=peer, device_id_type=MESH)

    def start(copies):
        for copy in copies:
            copy.start()

    def await_bytes(ref, sem):
        pltpu.make_async_copy(ref, ref, sem).wait()

    here = pl.ds(pl.multiple_of(h * PIECE, PIECE), PIECE)

    def target(c):
        owner = pair if c % 2 else x
        return owner, (owner if c >= 2 else NX - 1 - owner)

    def og_part(dz, c):
        column = (lax.rem(z + dz, NZ) * NX + target(c)[1]) * BLK
        return og_ref.at[
            pl.ds(pl.multiple_of(y * ROWS, ROWS), ROWS), pl.ds(pl.multiple_of(column, BLK), BLK)
        ]

    left_in = pltpu.make_async_copy(left_ref, stats.at[0, here], own_sem.at[2])
    right_in = pltpu.make_async_copy(right_ref, stats.at[1, here], own_sem.at[3])
    lroot_in = pltpu.make_async_copy(lroot_ref, lroot.at[here], own_sem.at[4])
    rroot_in = pltpu.make_async_copy(rroot_ref, rroot, own_sem.at[5])
    left_over = remote(left_ref, stats.at[0, here], s_send.at[0], s_recv.at[0], sibling)
    right_over = remote(right_ref, stats.at[1, here], s_send.at[1], s_recv.at[1], sibling)
    lroot_over = remote(lroot_ref, lroot.at[here], s_send.at[2], s_recv.at[2], sibling)
    rroot_over = remote(rroot, rroot, s_send.at[4], s_recv.at[4], sibling)

    def renew_left(grad):
        stats[0] = stats[0] + lax.dot_general(
            grad, grad, (((1,), (1,)), ((), ())), preferred_element_type=jnp.float32
        )
        lroot[...] = jnp.where(fresh[0, 0] > 0, inverse_root(stats[0]), lroot[...])

    g_copy = remote(grad_buf, grad_buf, s_send.at[3], s_recv.at[3], sibling)
    raw_in = pltpu.make_async_copy(act_ref, act_raw, own_sem.at[1])
    raw_in.start()
    raw_in.wait()
    act_own[...] = act_raw[...].T
    pl.semaphore_wait(barrier, len(peers))

    @pl.when(h == 0)
    def _():
        start(
            [
                remote(act_own, act_buf.at[0, SLOT[1], 0], a_send, a_recv.at[0], crossed(1)),
                remote(act_own, act_buf.at[0, SLOT[7], 0], a_send, a_recv.at[0], crossed(7)),
                remote(act_own, act_buf.at[0, 0, 0], a_send, a_recv.at[4], sibling),
            ]
        )
        for i, (c, first, end) in enumerate(STAGES):
            for slot in reversed(range(first, end)):
                if slot or c % 2:
                    remote(
                        og_part(ORDER[slot], c),
                        og_buf.at[c, slot, y],
                        z_send,
                        z_recv.at[i],
                        crossed(ORDER[slot], target(c)[0]),
                    ).start()
            if i == 0:
                remote(act_own, act_buf.at[1, 0, 0], a_send, x_recv, crossed(0, pair)).start()
        start([left_in, right_in, lroot_in, left_over, right_over, lroot_over])
        for copy in (left_in, right_in, lroot_in, left_over, lroot_over):
            copy.wait()
        stats[0] = decay_rate * stats[0]
        stats[1, here] = decay_rate * stats[1, here]
        g_copy.wait_recv()
        renew_left(grad_buf[...])
        rroot_over.wait_recv()

    @pl.when(h == 1)
    def _():
        own_og = [
            pltpu.make_async_copy(og_part(0, c), og_buf.at[c, 0, y], own_sem.at[c * 3])
            for c in (0, 2)
        ]

        def send_act(i):
            up, down = act_buf.at[0, SLOT[i]], act_buf.at[0, SLOT[-i % NZ]]
            if i < 4:
                to_up, to_down = act_buf.at[0, SLOT[i + 1]], act_buf.at[0, SLOT[7 - i]]
                if i == 3:
                    up, to_up, down, to_down = up.at[0], to_up.at[0], down.at[1], to_down.at[1]
                if i == 0:
                    up, to_up, down, to_down = act_own, to_up.at[1], act_own, to_down.at[1]
                start(
                    [
                        remote(up, to_up, a_send, a_recv.at[i], at(1)),
                        remote(down, to_down, a_send, a_recv.at[i], at(7)),
                    ]
                )
            if i == 0:
                remote(act_own, act_buf.at[1, 0, 1], x_send, x_recv, at(0, pair)).start()
                return
            for slot in (SLOT[i], SLOT[-i % NZ]) if i < 4 else (SLOT[i],):
                src, dst = act_buf.at[0, slot], act_buf.at[1, slot]
                remote(src, dst, x_send, x_recv, at(0, pair)).start()

        def next_act(i):
            await_bytes(act_buf.at[0, 0:2] if i < 4 else act_buf.at[0, 0], a_recv.at[i - 1])
            send_act(i)

        low, high = lax.rem(y + 3, NY), lax.rem(y + 1, NY)

        def first_y(i):
            c, first, end = STAGES[i]
            if c % 2 == 0:
                own_og[c // 2].wait()
            await_bytes(og_buf.at[c, first if c % 2 else first + 1 : end, 0], z_recv.at[i])
            mine = og_buf.at[c, first:end, y]
            start(
                [
                    remote(mine, mine, y_send, y_recv.at[i, 0], at_y(1)),
                    remote(mine, mine, y_send, y_recv.at[i, 0], at_y(3)),
                ]
            )

        def second_y(i):
            c, first, end = STAGES[i]
            await_bytes(og_buf.at[c, first:end, 0:2], y_recv.at[i, 0])
            middle = (first + end) // 2
            up, down = og_buf.at[c, first:middle, low], og_buf.at[c, middle:end, high]
            start(
                [
                    remote(up, up, y_send, y_recv.at[i, 1], at_y(1)),
                    remote(down, down, y_send, y_recv.at[i, 1], at_y(3)),
                ]
            )

        def product(i):
            c, first, end = STAGES[i]
            await_bytes(og_buf.at[c, first:end, 0], y_recv.at[i, 1])
            rows = og_buf[c, first:end].reshape((end - first) * TOKENS, BLK)
            blocks = [act_buf[c % 2, slot].reshape(BLK, TOKENS) for slot in range(first, end)]
            columns = jnp.concatenate(blocks, axis=1)
            return jnp.dot(columns, rows, preferred_element_type=jnp.float32)

        start(own_og)
        send_act(0)
        act_buf[0, 0, 1] = act_own[...]
        next_act(1)
        first_y(0)
        next_act(2)
        start([left_in, right_in, lroot_in, rroot_in, left_over, lroot_over])
        first_y(1)
        second_y(0)
        next_act(3)
        first_y(2)
        second_y(1)
        await_bytes(act_buf.at[0, 0, 0], a_recv.at[4])
        next_act(4)
        total[...] = product(0)
        first_y(3)
        second_y(2)
        await_bytes(act_buf.at[1], x_recv)
        part_out[...] = (total[...] + product(1)).astype(jnp.bfloat16)
        r_copy = remote(part_out, part_in, r_send, r_recv, at(0, partner))
        r_copy.start()
        for copy in (left_in, right_in, lroot_in, rroot_in, left_over, lroot_over):
            copy.wait()
        right_over.wait_recv()
        stats[...] = decay_rate * stats[...]
        first_y(4)
        second_y(3)
        total[...] = product(2)
        second_y(4)
        total[...] = total[...] + product(3)
        r_copy.wait_recv()
        total[...] = total[...] + part_in[...].astype(jnp.float32)
        grad_buf[...] = (total[...] + product(4)).astype(jnp.bfloat16)
        g_copy.start()
        grad = grad_buf[...]
        stats[1] = stats[1] + across_rows(grad, grad)
        rroot[...] = jnp.where(fresh[0, 0] > 0, inverse_root(stats[1]), rroot[...])
        rroot_over.start()
        renew_left(grad)

    grad = grad_buf[...]
    grad_wide = grad.astype(jnp.float32)
    grad_square = jnp.sum(grad_wide * grad_wide)
    right_copy = pltpu.make_async_copy(stats.at[1, here], right_new, out_sem.at[0])
    left_copy = pltpu.make_async_copy(stats.at[0, here], left_new, out_sem.at[1])
    left_copy.start()
    half = jnp.dot(lroot[...], grad, preferred_element_type=jnp.float32).astype(jnp.bfloat16)
    shaped[...] = jnp.dot(half, rroot[...], preferred_element_type=jnp.float32)
    entries = 1.0 / (BLK * BLK)
    ratio = jnp.sqrt(grad_square * entries + epsilon) / jnp.sqrt(
        jnp.sum(shaped[...] * shaped[...]) * entries + epsilon
    )
    piece[...] = (ratio * shaped[here]).astype(jnp.bfloat16)

    below, above = lax.rem(y + 3, NY), lax.rem(y + 1, NY)
    bottom, top = pl.ds(0, PIECE // 2), pl.ds(PIECE // 2, PIECE // 2)

    def spread(i, rows, owner, k):
        src = piece.at[rows] if owner is y else out.at[owner, rows]
        return remote(src, out.at[owner, rows], u_send.at[i], u_recv.at[i], at_y(k))

    first = [spread(0, bottom, y, 1), spread(1, top, y, 3)]
    rest = [spread(2, top, y, 1), spread(3, bottom, y, 3)]
    second = [spread(4, bottom, below, 1), spread(5, top, above, 3)]
    start(first + rest)
    own_copy = pltpu.make_async_copy(piece, out.at[y], out_sem.at[2])
    own_copy.start()

    @pl.when(h == 0)
    def _():
        stats[1, here] = stats[1, here] + across_rows(grad_buf[:, 0:PIECE], grad_buf[...])
        right_copy.start()
        right_over.wait_send()
        await_bytes(act_buf.at[0, 0:2], a_send)
        await_bytes(og_buf.at[0:3, 0:5, 0:2], z_send)

    @pl.when(h == 1)
    def _():
        right_copy.start()
        rroot_over.wait_send()
        await_bytes(act_buf.at[0, 0:6], a_send)
        await_bytes(og_buf.at[0:3, 0:5, 0:2], x_send)
        await_bytes(og_buf.at[:, :, 0:3], y_send)
        await_bytes(part_out, r_send)
        g_copy.wait_send()

    for one, two in zip(first, second):
        one.wait_recv()
        two.start()
    for copy in rest + second:
        copy.wait_recv()
    for copy in first + rest + second:
        copy.wait_send()
    for copy in (right_copy, left_copy, own_copy):
        copy.wait()


def step(fresh, act, og, left, right, lroot, rroot):
    hbm = pl.BlockSpec(memory_space=pl.ANY)
    dma = pltpu.SemaphoreType.DMA
    f32, b16 = jnp.float32, jnp.bfloat16
    return pl.pallas_call(
        step_kernel,
        out_shape=(
            pltpu.VMEM((NY, PIECE, BLK), b16),
            pltpu.VMEM((PIECE, BLK), f32),
            pltpu.VMEM((PIECE, BLK), f32),
        ),
        in_specs=[pl.BlockSpec(memory_space=pltpu.SMEM)] + [hbm] * 6,
        out_specs=(hbm,) * 3,
        scratch_shapes=[
            pltpu.VMEM((TOKENS, PIECE), b16),
            pltpu.VMEM((PIECE, TOKENS), b16),
            pltpu.VMEM((2, NZ, 2, PIECE, TOKENS), b16),
            pltpu.VMEM((4, NZ, NY, ROWS, BLK), b16),
            pltpu.VMEM((BLK, BLK), b16),
            pltpu.VMEM((BLK, BLK), b16),
            pltpu.VMEM((BLK, BLK), b16),
            pltpu.VMEM((2, BLK, BLK), f32),
            pltpu.VMEM((BLK, BLK), b16),
            pltpu.VMEM((BLK, BLK), b16),
            pltpu.VMEM((PIECE, BLK), b16),
            pltpu.VMEM((BLK, BLK), f32),
            pltpu.VMEM((BLK, BLK), f32),
            dma((7,)),
            dma,
            dma((5,)),
            dma,
            dma((5,)),
            dma,
            dma,
            dma,
            dma((5, 2)),
            dma,
            dma,
            dma((5,)),
            dma((5,)),
            dma((6,)),
            dma((6,)),
            dma((3,)),
        ],
        compiler_params=pltpu.CompilerParams(
            collective_id=0, has_side_effects=True, vmem_limit_bytes=VMEM_LIMIT
        ),
        name="step",
    )(fresh, act, og, left, right, lroot, rroot)


def finish_kernel(update, left, right, update_out, left_out, right_out, sems):
    copies = [
        pltpu.make_async_copy(update, update_out, sems.at[0]),
        pltpu.make_async_copy(left, left_out, sems.at[1]),
        pltpu.make_async_copy(right, right_out, sems.at[2]),
    ]
    for copy in copies:
        copy.start()
    for copy in copies:
        copy.wait()


def finish(*arrays):
    vmem = pl.BlockSpec(memory_space=pltpu.VMEM)
    anywhere = pl.BlockSpec(memory_space=pl.ANY)
    return pl.pallas_call(
        finish_kernel,
        out_shape=tuple(jax.ShapeDtypeStruct(a.shape, a.dtype) for a in arrays),
        in_specs=[vmem] * 3,
        out_specs=(anywhere,) * 3,
        scratch_shapes=[pltpu.SemaphoreType.DMA((3,))],
        compiler_params=pltpu.CompilerParams(vmem_limit_bytes=4 * 2**20),
        name="finish",
    )(*arrays)


def shards(act, og, left_state, right_state, left_root_old, right_root_old, refresh):
    update, left_new, right_new = finish(
        *step(
            refresh,
            act,
            og,
            left_state[0, 0],
            right_state[0, 0],
            left_root_old[0, 0],
            right_root_old[0, 0],
        )
    )
    return update[:, None], left_new[None, None], right_new[None, None]


def solution(mesh):
    placed = (
        P("dp", ("mp", "helper")),
        P("dp", None),
        P("mp", "dp", "helper", None),
        P("mp", "dp", "helper", None),
        P("mp", "dp", "helper", None),
        P("mp", "dp", None, None),
        P("mp", "dp"),
    )
    return jax.shard_map(
        shards,
        mesh=mesh,
        in_specs=placed,
        out_specs=(
            P(None, "helper", None, "dp"),
            P("mp", "dp", "helper", None),
            P("mp", "dp", "helper", None),
        ),
        check_vma=False,
    )
```

```python
import jax
import jax.numpy as jnp
from jax import lax
from jax.experimental import pallas as pl
from jax.experimental.pallas import tpu as pltpu
from jax.sharding import PartitionSpec as P

decay_rate = 0.95
epsilon = 1e-06

NZ, NX, NY = 8, 4, 4
BLK = 512
PIECE = 256
TOKENS = 128
ROWS = 32
ORDER = (0, 1, 7, 2, 6, 3, 5, 4)
SLOT = {distance: slot for slot, distance in enumerate(ORDER)}
REACH = {1: 5, -1: 2}
STAGES = ((0, 0, 8), (1, 0, 8), (2, 0, 8), (3, 0, 4), (3, 4, 8))
VMEM_LIMIT = 56 * 2**20
MESH = pl.DeviceIdType.MESH


def place():
    d = lax.axis_index("dp")
    return d // NX, d % NX, lax.axis_index("mp"), lax.axis_index("helper")


def remote(src, dst, send, recv, device):
    return pltpu.make_async_remote_copy(
        src_ref=src,
        dst_ref=dst,
        send_sem=send,
        recv_sem=recv,
        device_id=device,
        device_id_type=MESH,
    )


def across_rows(a, b):
    return lax.dot_general(a, b, (((0,), (0,)), ((), ())), preferred_element_type=jnp.float32)


def inverse_root(s):
    b16 = jnp.bfloat16
    scale = BLK * jnp.sqrt(jnp.sum(s * s) * (1.0 / (BLK * BLK)) + epsilon)
    first = s * (1.0 / scale)
    first16 = first.astype(b16)
    second = jnp.dot(first16, first16, preferred_element_type=jnp.float32)
    third = jnp.dot(second.astype(b16), first16, preferred_element_type=jnp.float32)
    upper = (250.0 / 4096) * first - (25.0 / 4096) * second + (1.0 / 4096) * third
    high = jnp.dot(third.astype(b16), upper.astype(b16), preferred_element_type=jnp.float32)
    rows = lax.broadcasted_iota(jnp.int32, s.shape, 0)
    columns = lax.broadcasted_iota(jnp.int32, s.shape, 1)
    constant = jnp.where(rows == columns, 25.0 / 16, 0.0)
    low = (-5.0 / 16 - 3125.0 / 4096) * first + (3125.0 / 4096) * second - (1250.0 / 4096) * third
    return ((constant + low + high) * lax.rsqrt(jnp.sqrt(scale))).astype(b16)


def step_kernel(
    fresh,
    act_ref,
    og_ref,
    left_ref,
    right_ref,
    lroot_ref,
    rroot_ref,
    out,
    left_new,
    right_new,
    act_raw,
    act_own,
    act_buf,
    og_buf,
    part_out,
    part_in,
    grad_buf,
    stats,
    lroot,
    rroot,
    piece,
    shaped,
    total,
    own_sem,
    z_send,
    z_recv,
    a_send,
    a_recv,
    x_send,
    x_recv,
    y_send,
    y_recv,
    r_send,
    r_recv,
    s_send,
    s_recv,
    u_send,
    u_recv,
    out_sem,
):
    z, x, y, h = place()

    pair = x + 1 - 2 * lax.rem(x, 2)
    partner = NX - 1 - x

    def at(dz, column=x):
        return (lax.rem(z + dz, NZ) * NX + column, y, h)

    def crossed(dz, column=x):
        return (lax.rem(z + dz, NZ) * NX + column, y, 1 - h)

    def at_y(k):
        return (z * NX + x, lax.rem(y + k, NY), h)

    sibling = crossed(0)
    barrier = pltpu.get_barrier_semaphore()
    peers = [crossed(dz) for dz in range(NZ)] + [crossed(dz, pair) for dz in range(NZ)]
    peers += [at(1), at(7), at(0, pair), at(0, partner), at_y(1), at_y(3)]
    for peer in peers:
        pl.semaphore_signal(barrier, inc=1, device_id=peer, device_id_type=MESH)

    def start(copies):
        for copy in copies:
            copy.start()

    def await_bytes(ref, sem):
        pltpu.make_async_copy(ref, ref, sem).wait()

    here = pl.ds(pl.multiple_of(h * PIECE, PIECE), PIECE)

    def target(c):
        owner = pair if c % 2 else x
        return owner, (owner if c >= 2 else NX - 1 - owner)

    def og_part(dz, c):
        column = (lax.rem(z + dz, NZ) * NX + target(c)[1]) * BLK
        return og_ref.at[
            pl.ds(pl.multiple_of(y * ROWS, ROWS), ROWS), pl.ds(pl.multiple_of(column, BLK), BLK)
        ]

    left_in = pltpu.make_async_copy(left_ref, stats.at[0, here], own_sem.at[2])
    right_in = pltpu.make_async_copy(right_ref, stats.at[1, here], own_sem.at[3])
    lroot_in = pltpu.make_async_copy(lroot_ref, lroot.at[here], own_sem.at[4])
    rroot_in = pltpu.make_async_copy(rroot_ref, rroot, own_sem.at[5])
    left_over = remote(left_ref, stats.at[0, here], s_send.at[0], s_recv.at[0], sibling)
    right_over = remote(right_ref, stats.at[1, here], s_send.at[1], s_recv.at[1], sibling)
    lroot_over = remote(lroot_ref, lroot.at[here], s_send.at[2], s_recv.at[2], sibling)
    rroot_over = remote(rroot, rroot, s_send.at[4], s_recv.at[4], sibling)

    def renew_left(grad):
        stats[0] = stats[0] + lax.dot_general(
            grad, grad, (((1,), (1,)), ((), ())), preferred_element_type=jnp.float32
        )
        lroot[...] = jnp.where(fresh[0, 0] > 0, inverse_root(stats[0]), lroot[...])

    g_copy = remote(grad_buf, grad_buf, s_send.at[3], s_recv.at[3], sibling)
    raw_in = pltpu.make_async_copy(act_ref, act_raw, own_sem.at[1])
    raw_in.start()
    pl.semaphore_wait(barrier, len(peers))

    @pl.when(h == 0)
    def _():
        for i, (c, first, end) in enumerate(STAGES):
            for slot in reversed(range(first, end)):
                if slot or c % 2:
                    remote(
                        og_part(ORDER[slot], c),
                        og_buf.at[c, slot, y],
                        z_send,
                        z_recv.at[i],
                        crossed(ORDER[slot], target(c)[0]),
                    ).start()
            if i == 0:
                raw_in.wait()
                act_own[...] = act_raw[...].T
                start(
                    [
                        remote(act_own, act_buf.at[0, SLOT[1], 0], a_send, a_recv.at[0], crossed(1)),
                        remote(act_own, act_buf.at[0, SLOT[7], 0], a_send, a_recv.at[0], crossed(7)),
                        remote(act_own, act_buf.at[0, 0, 0], a_send, a_recv.at[5], sibling),
                        remote(act_own, act_buf.at[1, 0, 0], a_send, x_recv, crossed(0, pair)),
                    ]
                )
        start([left_in, right_in, lroot_in, left_over, right_over, lroot_over])
        for copy in (left_in, right_in, lroot_in, left_over, lroot_over):
            copy.wait()
        stats[0] = decay_rate * stats[0]
        stats[1, here] = decay_rate * stats[1, here]
        g_copy.wait_recv()
        renew_left(grad_buf[...])
        rroot_over.wait_recv()

    @pl.when(h == 1)
    def _():
        own_og = [
            pltpu.make_async_copy(og_part(0, c), og_buf.at[c, 0, y], own_sem.at[c * 3])
            for c in (0, 2)
        ]

        def send_act(i):
            source = act_own if i == 0 else None
            for way in (1, -1):
                distance = way * i
                if i < REACH[way]:
                    src = source if i == 0 else act_buf.at[0, SLOT[distance % NZ]]
                    dst = act_buf.at[0, SLOT[(distance + way) % NZ]]
                    if i == 0:
                        dst = dst.at[1]
                    remote(src, dst, a_send, a_recv.at[i], at(way % NZ)).start()
                if 0 < i <= REACH[way]:
                    slot = SLOT[distance % NZ]
                    remote(
                        act_buf.at[0, slot], act_buf.at[1, slot], x_send, x_recv, at(0, pair)
                    ).start()
            if i == 0:
                remote(act_own, act_buf.at[1, 0, 1], x_send, x_recv, at(0, pair)).start()

        def next_act(i):
            chunks = sum(i <= reach for reach in REACH.values())
            await_bytes(act_buf.at[0, 0:chunks], a_recv.at[i - 1])
            send_act(i)

        low, high = lax.rem(y + 3, NY), lax.rem(y + 1, NY)

        def first_y(i):
            c, first, end = STAGES[i]
            if c % 2 == 0:
                own_og[c // 2].wait()
            await_bytes(og_buf.at[c, first if c % 2 else first + 1 : end, 0], z_recv.at[i])
            mine = og_buf.at[c, first:end, y]
            start(
                [
                    remote(mine, mine, y_send, y_recv.at[i, 0], at_y(1)),
                    remote(mine, mine, y_send, y_recv.at[i, 0], at_y(3)),
                ]
            )

        def second_y(i):
            c, first, end = STAGES[i]
            await_bytes(og_buf.at[c, first:end, 0:2], y_recv.at[i, 0])
            middle = (first + end) // 2
            up, down = og_buf.at[c, first:middle, low], og_buf.at[c, middle:end, high]
            start(
                [
                    remote(up, up, y_send, y_recv.at[i, 1], at_y(1)),
                    remote(down, down, y_send, y_recv.at[i, 1], at_y(3)),
                ]
            )

        def product(i):
            c, first, end = STAGES[i]
            await_bytes(og_buf.at[c, first:end, 0], y_recv.at[i, 1])
            rows = og_buf[c, first:end].reshape((end - first) * TOKENS, BLK)
            blocks = [act_buf[c % 2, slot].reshape(BLK, TOKENS) for slot in range(first, end)]
            columns = jnp.concatenate(blocks, axis=1)
            return jnp.dot(columns, rows, preferred_element_type=jnp.float32)

        start(own_og)
        raw_in.wait()
        act_own[...] = act_raw[...].T
        send_act(0)
        act_buf[0, 0, 1] = act_own[...]
        next_act(1)
        first_y(0)
        next_act(2)
        start([left_in, right_in, lroot_in, rroot_in, left_over, lroot_over])
        first_y(1)
        second_y(0)
        next_act(3)
        first_y(2)
        second_y(1)
        await_bytes(act_buf.at[0, 0, 0], a_recv.at[5])
        next_act(4)
        first_y(3)
        next_act(5)
        total[...] = product(0)
        second_y(2)
        await_bytes(act_buf.at[1], x_recv)
        part_out[...] = (total[...] + product(1)).astype(jnp.bfloat16)
        r_copy = remote(part_out, part_in, r_send, r_recv, at(0, partner))
        r_copy.start()
        for copy in (left_in, right_in, lroot_in, rroot_in, left_over, lroot_over):
            copy.wait()
        right_over.wait_recv()
        stats[...] = decay_rate * stats[...]
        first_y(4)
        second_y(3)
        total[...] = product(2)
        second_y(4)
        total[...] = total[...] + product(3)
        r_copy.wait_recv()
        total[...] = total[...] + part_in[...].astype(jnp.float32)
        grad_buf[...] = (total[...] + product(4)).astype(jnp.bfloat16)
        g_copy.start()
        grad = grad_buf[...]
        stats[1] = stats[1] + across_rows(grad, grad)
        rroot[...] = jnp.where(fresh[0, 0] > 0, inverse_root(stats[1]), rroot[...])
        rroot_over.start()
        renew_left(grad)

    grad = grad_buf[...]
    grad_wide = grad.astype(jnp.float32)
    grad_square = jnp.sum(grad_wide * grad_wide)
    right_copy = pltpu.make_async_copy(stats.at[1, here], right_new, out_sem.at[0])
    left_copy = pltpu.make_async_copy(stats.at[0, here], left_new, out_sem.at[1])
    left_copy.start()
    half = jnp.dot(lroot[...], grad, preferred_element_type=jnp.float32).astype(jnp.bfloat16)
    shaped[...] = jnp.dot(half, rroot[...], preferred_element_type=jnp.float32)
    entries = 1.0 / (BLK * BLK)
    ratio = jnp.sqrt(grad_square * entries + epsilon) / jnp.sqrt(
        jnp.sum(shaped[...] * shaped[...]) * entries + epsilon
    )
    piece[...] = (ratio * shaped[here]).astype(jnp.bfloat16)

    below, above = lax.rem(y + 3, NY), lax.rem(y + 1, NY)
    bottom, top = pl.ds(0, PIECE // 2), pl.ds(PIECE // 2, PIECE // 2)

    def spread(i, rows, owner, k):
        src = piece.at[rows] if owner is y else out.at[owner, rows]
        return remote(src, out.at[owner, rows], u_send.at[i], u_recv.at[i], at_y(k))

    first = [spread(0, bottom, y, 1), spread(1, top, y, 3)]
    rest = [spread(2, top, y, 1), spread(3, bottom, y, 3)]
    second = [spread(4, bottom, below, 1), spread(5, top, above, 3)]
    start(first + rest)
    own_copy = pltpu.make_async_copy(piece, out.at[y], out_sem.at[2])
    own_copy.start()

    @pl.when(h == 0)
    def _():
        stats[1, here] = stats[1, here] + across_rows(grad_buf[:, 0:PIECE], grad_buf[...])
        right_copy.start()
        right_over.wait_send()
        await_bytes(act_buf.at[0, 0:2], a_send)
        await_bytes(og_buf.at[0:3, 0:5, 0:2], z_send)

    @pl.when(h == 1)
    def _():
        right_copy.start()
        rroot_over.wait_send()
        await_bytes(act_buf.at[0, 0:6], a_send)
        await_bytes(og_buf.at[0:3, 0:5, 0:2], x_send)
        await_bytes(og_buf.at[:, :, 0:3], y_send)
        await_bytes(part_out, r_send)
        g_copy.wait_send()

    for one, two in zip(first, second):
        one.wait_recv()
        two.start()
    for copy in rest + second:
        copy.wait_recv()
    for copy in first + rest + second:
        copy.wait_send()
    for copy in (right_copy, left_copy, own_copy):
        copy.wait()


def step(fresh, act, og, left, right, lroot, rroot):
    hbm = pl.BlockSpec(memory_space=pl.ANY)
    dma = pltpu.SemaphoreType.DMA
    f32, b16 = jnp.float32, jnp.bfloat16
    return pl.pallas_call(
        step_kernel,
        out_shape=(
            pltpu.VMEM((NY, PIECE, BLK), b16),
            pltpu.VMEM((PIECE, BLK), f32),
            pltpu.VMEM((PIECE, BLK), f32),
        ),
        in_specs=[pl.BlockSpec(memory_space=pltpu.SMEM)] + [hbm] * 6,
        out_specs=(hbm,) * 3,
        scratch_shapes=[
            pltpu.VMEM((TOKENS, PIECE), b16),
            pltpu.VMEM((PIECE, TOKENS), b16),
            pltpu.VMEM((2, NZ, 2, PIECE, TOKENS), b16),
            pltpu.VMEM((4, NZ, NY, ROWS, BLK), b16),
            pltpu.VMEM((BLK, BLK), b16),
            pltpu.VMEM((BLK, BLK), b16),
            pltpu.VMEM((BLK, BLK), b16),
            pltpu.VMEM((2, BLK, BLK), f32),
            pltpu.VMEM((BLK, BLK), b16),
            pltpu.VMEM((BLK, BLK), b16),
            pltpu.VMEM((PIECE, BLK), b16),
            pltpu.VMEM((BLK, BLK), f32),
            pltpu.VMEM((BLK, BLK), f32),
            dma((7,)),
            dma,
            dma((5,)),
            dma,
            dma((6,)),
            dma,
            dma,
            dma,
            dma((5, 2)),
            dma,
            dma,
            dma((5,)),
            dma((5,)),
            dma((6,)),
            dma((6,)),
            dma((3,)),
        ],
        compiler_params=pltpu.CompilerParams(
            collective_id=0, has_side_effects=True, vmem_limit_bytes=VMEM_LIMIT
        ),
        name="step",
    )(fresh, act, og, left, right, lroot, rroot)


def finish_kernel(update, left, right, update_out, left_out, right_out, sems):
    copies = [
        pltpu.make_async_copy(update, update_out, sems.at[0]),
        pltpu.make_async_copy(left, left_out, sems.at[1]),
        pltpu.make_async_copy(right, right_out, sems.at[2]),
    ]
    for copy in copies:
        copy.start()
    for copy in copies:
        copy.wait()


def finish(*arrays):
    vmem = pl.BlockSpec(memory_space=pltpu.VMEM)
    anywhere = pl.BlockSpec(memory_space=pl.ANY)
    return pl.pallas_call(
        finish_kernel,
        out_shape=tuple(jax.ShapeDtypeStruct(a.shape, a.dtype) for a in arrays),
        in_specs=[vmem] * 3,
        out_specs=(anywhere,) * 3,
        scratch_shapes=[pltpu.SemaphoreType.DMA((3,))],
        compiler_params=pltpu.CompilerParams(vmem_limit_bytes=4 * 2**20),
        name="finish",
    )(*arrays)


def shards(act, og, left_state, right_state, left_root_old, right_root_old, refresh):
    update, left_new, right_new = finish(
        *step(
            refresh,
            act,
            og,
            left_state[0, 0],
            right_state[0, 0],
            left_root_old[0, 0],
            right_root_old[0, 0],
        )
    )
    return update[:, None], left_new[None, None], right_new[None, None]


def solution(mesh):
    placed = (
        P("dp", ("mp", "helper")),
        P("dp", None),
        P("mp", "dp", "helper", None),
        P("mp", "dp", "helper", None),
        P("mp", "dp", "helper", None),
        P("mp", "dp", None, None),
        P("mp", "dp"),
    )
    return jax.shard_map(
        shards,
        mesh=mesh,
        in_specs=placed,
        out_specs=(
            P(None, "helper", None, "dp"),
            P("mp", "dp", "helper", None),
            P("mp", "dp", "helper", None),
        ),
        check_vma=False,
    )
```

```python
import jax
import jax.numpy as jnp
from jax import lax
from jax.experimental import pallas as pl
from jax.experimental.pallas import tpu as pltpu
from jax.sharding import PartitionSpec as P

decay_rate = 0.95
epsilon = 1e-06

NZ, NX, NY = 8, 4, 4
BLK = 512
PIECE = 256
TOKENS = 128
ROWS = 32
ORDER = (0, 1, 7, 2, 6, 3, 5, 4)
SLOT = {distance: slot for slot, distance in enumerate(ORDER)}
NEAR = (1, 7, 2, 6)
STAGES = ((0, 0, 8), (1, 0, 8), (2, 0, 8), (3, 0, 4), (3, 4, 8))
VMEM_LIMIT = 56 * 2**20
MESH = pl.DeviceIdType.MESH


def place():
    d = lax.axis_index("dp")
    return d // NX, d % NX, lax.axis_index("mp"), lax.axis_index("helper")


def remote(src, dst, send, recv, device):
    return pltpu.make_async_remote_copy(
        src_ref=src,
        dst_ref=dst,
        send_sem=send,
        recv_sem=recv,
        device_id=device,
        device_id_type=MESH,
    )


def across_rows(a, b):
    return lax.dot_general(a, b, (((0,), (0,)), ((), ())), preferred_element_type=jnp.float32)


def inverse_root(s):
    b16 = jnp.bfloat16
    scale = BLK * jnp.sqrt(jnp.sum(s * s) * (1.0 / (BLK * BLK)) + epsilon)
    first = s * (1.0 / scale)
    first16 = first.astype(b16)
    second = jnp.dot(first16, first16, preferred_element_type=jnp.float32)
    third = jnp.dot(second.astype(b16), first16, preferred_element_type=jnp.float32)
    upper = (250.0 / 4096) * first - (25.0 / 4096) * second + (1.0 / 4096) * third
    high = jnp.dot(third.astype(b16), upper.astype(b16), preferred_element_type=jnp.float32)
    rows = lax.broadcasted_iota(jnp.int32, s.shape, 0)
    columns = lax.broadcasted_iota(jnp.int32, s.shape, 1)
    constant = jnp.where(rows == columns, 25.0 / 16, 0.0)
    low = (-5.0 / 16 - 3125.0 / 4096) * first + (3125.0 / 4096) * second - (1250.0 / 4096) * third
    return ((constant + low + high) * lax.rsqrt(jnp.sqrt(scale))).astype(b16)


def step_kernel(
    fresh,
    act_ref,
    og_ref,
    left_ref,
    right_ref,
    lroot_ref,
    rroot_ref,
    out,
    left_new,
    right_new,
    act_raw,
    act_own,
    act_buf,
    og_buf,
    part_out,
    part_in,
    grad_buf,
    stats,
    lroot,
    rroot,
    piece,
    shaped,
    total,
    own_sem,
    z_send,
    z_recv,
    a_send,
    a_recv,
    x_send,
    x_recv,
    y_send,
    y_recv,
    r_send,
    r_recv,
    s_send,
    s_recv,
    u_send,
    u_recv,
    out_sem,
):
    z, x, y, h = place()

    pair = x + 1 - 2 * lax.rem(x, 2)
    partner = NX - 1 - x

    def at(dz, column=x):
        return (lax.rem(z + dz, NZ) * NX + column, y, h)

    def crossed(dz, column=x):
        return (lax.rem(z + dz, NZ) * NX + column, y, 1 - h)

    def at_y(k):
        return (z * NX + x, lax.rem(y + k, NY), h)

    raw_in = pltpu.make_async_copy(act_ref, act_raw, own_sem.at[1])
    raw_in.start()
    sibling = crossed(0)
    barrier = pltpu.get_barrier_semaphore()
    peers = [crossed(dz) for dz in range(NZ)] + [crossed(dz, pair) for dz in range(NZ)]
    peers += [at(dz) for dz in NEAR] + [at(0, pair), at(0, partner), at_y(1), at_y(3)]
    for peer in peers:
        pl.semaphore_signal(barrier, inc=1, device_id=peer, device_id_type=MESH)

    def start(copies):
        for copy in copies:
            copy.start()

    def await_bytes(ref, sem):
        pltpu.make_async_copy(ref, ref, sem).wait()

    here = pl.ds(pl.multiple_of(h * PIECE, PIECE), PIECE)

    def target(c):
        owner = pair if c % 2 else x
        return owner, (owner if c >= 2 else NX - 1 - owner)

    def og_part(dz, c):
        column = (lax.rem(z + dz, NZ) * NX + target(c)[1]) * BLK
        return og_ref.at[
            pl.ds(pl.multiple_of(y * ROWS, ROWS), ROWS), pl.ds(pl.multiple_of(column, BLK), BLK)
        ]

    left_in = pltpu.make_async_copy(left_ref, stats.at[0, here], own_sem.at[2])
    right_in = pltpu.make_async_copy(right_ref, stats.at[1, here], own_sem.at[3])
    lroot_in = pltpu.make_async_copy(lroot_ref, lroot.at[here], own_sem.at[4])
    rroot_in = pltpu.make_async_copy(rroot_ref, rroot, own_sem.at[5])
    left_over = remote(left_ref, stats.at[0, here], s_send.at[0], s_recv.at[0], sibling)
    right_over = remote(right_ref, stats.at[1, here], s_send.at[1], s_recv.at[1], sibling)
    lroot_over = remote(lroot_ref, lroot.at[here], s_send.at[2], s_recv.at[2], sibling)
    rroot_over = remote(rroot, rroot, s_send.at[4], s_recv.at[4], sibling)

    def renew_left(grad):
        stats[0] = stats[0] + lax.dot_general(
            grad, grad, (((1,), (1,)), ((), ())), preferred_element_type=jnp.float32
        )
        lroot[...] = jnp.where(fresh[0, 0] > 0, inverse_root(stats[0]), lroot[...])

    g_copy = remote(grad_buf, grad_buf, s_send.at[3], s_recv.at[3], sibling)
    raw_in.wait()
    act_own[...] = act_raw[...].T
    pl.semaphore_wait(barrier, len(peers))

    @pl.when(h == 0)
    def _():
        for dz in NEAR:
            dst = act_buf.at[0, SLOT[dz], 0]
            remote(act_own, dst, a_send, a_recv.at[0], crossed(dz)).start()
        remote(act_own, act_buf.at[0, 0, 0], a_send, a_recv.at[2], sibling).start()
        remote(act_own, act_buf.at[1, 0, 0], a_send, x_recv, crossed(0, pair)).start()
        for i, (c, first, end) in enumerate(STAGES):
            for slot in reversed(range(first, end)):
                if slot or c % 2:
                    remote(
                        og_part(ORDER[slot], c),
                        og_buf.at[c, slot, y],
                        z_send,
                        z_recv.at[i],
                        crossed(ORDER[slot], target(c)[0]),
                    ).start()
        start([left_in, right_in, lroot_in, left_over, right_over, lroot_over])
        for copy in (left_in, right_in, lroot_in, left_over, lroot_over):
            copy.wait()
        stats[0] = decay_rate * stats[0]
        stats[1, here] = decay_rate * stats[1, here]
        g_copy.wait_recv()
        renew_left(grad_buf[...])
        rroot_over.wait_recv()

    @pl.when(h == 1)
    def _():
        own_og = [
            pltpu.make_async_copy(og_part(0, c), og_buf.at[c, 0, y], own_sem.at[c * 3])
            for c in (0, 2)
        ]

        def exchange(distances):
            for distance in distances:
                slot = SLOT[distance]
                src, dst = act_buf.at[0, slot], act_buf.at[1, slot]
                remote(src, dst, x_send, x_recv, at(0, pair)).start()

        def pass_act():
            await_bytes(act_buf.at[0, 0:4], a_recv.at[0])
            for distance, half in ((2, 0), (6, 1)):
                way = distance // 2 if distance == 2 else 7
                chunk = act_buf.at[0, SLOT[distance]]
                middle = act_buf.at[0, SLOT[4], half]
                beyond = act_buf.at[0, SLOT[3 if distance == 2 else 5]]
                remote(chunk.at[half], middle, a_send, a_recv.at[1], at(distance)).start()
                remote(chunk, beyond, a_send, a_recv.at[1], at(way)).start()
            exchange(NEAR)

        low, high = lax.rem(y + 3, NY), lax.rem(y + 1, NY)

        def first_y(i):
            c, first, end = STAGES[i]
            if c % 2 == 0:
                own_og[c // 2].wait()
            await_bytes(og_buf.at[c, first if c % 2 else first + 1 : end, 0], z_recv.at[i])
            mine = og_buf.at[c, first:end, y]
            start(
                [
                    remote(mine, mine, y_send, y_recv.at[i, 0], at_y(1)),
                    remote(mine, mine, y_send, y_recv.at[i, 0], at_y(3)),
                ]
            )

        def second_y(i):
            c, first, end = STAGES[i]
            await_bytes(og_buf.at[c, first:end, 0:2], y_recv.at[i, 0])
            middle = (first + end) // 2
            up, down = og_buf.at[c, first:middle, low], og_buf.at[c, middle:end, high]
            start(
                [
                    remote(up, up, y_send, y_recv.at[i, 1], at_y(1)),
                    remote(down, down, y_send, y_recv.at[i, 1], at_y(3)),
                ]
            )

        def product(i):
            c, first, end = STAGES[i]
            await_bytes(og_buf.at[c, first:end, 0], y_recv.at[i, 1])
            rows = og_buf[c, first:end].reshape((end - first) * TOKENS, BLK)
            blocks = [act_buf[c % 2, slot].reshape(BLK, TOKENS) for slot in range(first, end)]
            columns = jnp.concatenate(blocks, axis=1)
            return jnp.dot(columns, rows, preferred_element_type=jnp.float32)

        for dz in NEAR:
            dst = act_buf.at[0, SLOT[dz], 1]
            remote(act_own, dst, a_send, a_recv.at[0], at(dz)).start()
        remote(act_own, act_buf.at[1, 0, 1], x_send, x_recv, at(0, pair)).start()
        start(own_og)
        act_buf[0, 0, 1] = act_own[...]
        pass_act()
        start([left_in, right_in, lroot_in, rroot_in, left_over, lroot_over])
        first_y(0)
        first_y(1)
        second_y(0)
        await_bytes(act_buf.at[0, 0:3], a_recv.at[1])
        exchange((3, 5, 4))
        first_y(2)
        second_y(1)
        await_bytes(act_buf.at[0, 0, 0], a_recv.at[2])
        total[...] = product(0)
        first_y(3)
        second_y(2)
        await_bytes(act_buf.at[1], x_recv)
        part_out[...] = (total[...] + product(1)).astype(jnp.bfloat16)
        r_copy = remote(part_out, part_in, r_send, r_recv, at(0, partner))
        r_copy.start()
        for copy in (left_in, right_in, lroot_in, rroot_in, left_over, lroot_over):
            copy.wait()
        right_over.wait_recv()
        stats[...] = decay_rate * stats[...]
        first_y(4)
        second_y(3)
        total[...] = product(2)
        second_y(4)
        total[...] = total[...] + product(3)
        r_copy.wait_recv()
        total[...] = total[...] + part_in[...].astype(jnp.float32)
        grad_buf[...] = (total[...] + product(4)).astype(jnp.bfloat16)
        g_copy.start()
        grad = grad_buf[...]
        stats[1] = stats[1] + across_rows(grad, grad)
        rroot[...] = jnp.where(fresh[0, 0] > 0, inverse_root(stats[1]), rroot[...])
        rroot_over.start()
        renew_left(grad)

    grad = grad_buf[...]
    grad_wide = grad.astype(jnp.float32)
    grad_square = jnp.sum(grad_wide * grad_wide)
    right_copy = pltpu.make_async_copy(stats.at[1, here], right_new, out_sem.at[0])
    left_copy = pltpu.make_async_copy(stats.at[0, here], left_new, out_sem.at[1])
    left_copy.start()
    half = jnp.dot(lroot[...], grad, preferred_element_type=jnp.float32).astype(jnp.bfloat16)
    shaped[...] = jnp.dot(half, rroot[...], preferred_element_type=jnp.float32)
    entries = 1.0 / (BLK * BLK)
    ratio = jnp.sqrt(grad_square * entries + epsilon) / jnp.sqrt(
        jnp.sum(shaped[...] * shaped[...]) * entries + epsilon
    )
    piece[...] = (ratio * shaped[here]).astype(jnp.bfloat16)

    below, above = lax.rem(y + 3, NY), lax.rem(y + 1, NY)
    bottom, top = pl.ds(0, PIECE // 2), pl.ds(PIECE // 2, PIECE // 2)

    def spread(i, rows, owner, k):
        src = piece.at[rows] if owner is y else out.at[owner, rows]
        return remote(src, out.at[owner, rows], u_send.at[i], u_recv.at[i], at_y(k))

    first = [spread(0, bottom, y, 1), spread(1, top, y, 3)]
    rest = [spread(2, top, y, 1), spread(3, bottom, y, 3)]
    second = [spread(4, bottom, below, 1), spread(5, top, above, 3)]
    start(first + rest)
    own_copy = pltpu.make_async_copy(piece, out.at[y], out_sem.at[2])
    own_copy.start()

    @pl.when(h == 0)
    def _():
        stats[1, here] = stats[1, here] + across_rows(grad_buf[:, 0:PIECE], grad_buf[...])
        right_copy.start()
        right_over.wait_send()
        await_bytes(act_buf.at[0, 0:3], a_send)
        await_bytes(og_buf.at[0:3, 0:5, 0:2], z_send)

    @pl.when(h == 1)
    def _():
        right_copy.start()
        rroot_over.wait_send()
        await_bytes(og_buf.at[0, 0:5, 0:4], a_send)
        await_bytes(og_buf.at[0:3, 0:5, 0:2], x_send)
        await_bytes(og_buf.at[:, :, 0:3], y_send)
        await_bytes(part_out, r_send)
        g_copy.wait_send()

    for one, two in zip(first, second):
        one.wait_recv()
        two.start()
    for copy in rest + second:
        copy.wait_recv()
    for copy in first + rest + second:
        copy.wait_send()
    for copy in (right_copy, left_copy, own_copy):
        copy.wait()


def step(fresh, act, og, left, right, lroot, rroot):
    hbm = pl.BlockSpec(memory_space=pl.ANY)
    dma = pltpu.SemaphoreType.DMA
    f32, b16 = jnp.float32, jnp.bfloat16
    return pl.pallas_call(
        step_kernel,
        out_shape=(
            pltpu.VMEM((NY, PIECE, BLK), b16),
            pltpu.VMEM((PIECE, BLK), f32),
            pltpu.VMEM((PIECE, BLK), f32),
        ),
        in_specs=[pl.BlockSpec(memory_space=pltpu.SMEM)] + [hbm] * 6,
        out_specs=(hbm,) * 3,
        scratch_shapes=[
            pltpu.VMEM((TOKENS, PIECE), b16),
            pltpu.VMEM((PIECE, TOKENS), b16),
            pltpu.VMEM((2, NZ, 2, PIECE, TOKENS), b16),
            pltpu.VMEM((4, NZ, NY, ROWS, BLK), b16),
            pltpu.VMEM((BLK, BLK), b16),
            pltpu.VMEM((BLK, BLK), b16),
            pltpu.VMEM((BLK, BLK), b16),
            pltpu.VMEM((2, BLK, BLK), f32),
            pltpu.VMEM((BLK, BLK), b16),
            pltpu.VMEM((BLK, BLK), b16),
            pltpu.VMEM((PIECE, BLK), b16),
            pltpu.VMEM((BLK, BLK), f32),
            pltpu.VMEM((BLK, BLK), f32),
            dma((7,)),
            dma,
            dma((5,)),
            dma,
            dma((5,)),
            dma,
            dma,
            dma,
            dma((5, 2)),
            dma,
            dma,
            dma((5,)),
            dma((5,)),
            dma((6,)),
            dma((6,)),
            dma((3,)),
        ],
        compiler_params=pltpu.CompilerParams(
            collective_id=0, has_side_effects=True, vmem_limit_bytes=VMEM_LIMIT
        ),
        name="step",
    )(fresh, act, og, left, right, lroot, rroot)


def finish_kernel(update, left, right, update_out, left_out, right_out, sems):
    copies = [
        pltpu.make_async_copy(update, update_out, sems.at[0]),
        pltpu.make_async_copy(left, left_out, sems.at[1]),
        pltpu.make_async_copy(right, right_out, sems.at[2]),
    ]
    for copy in copies:
        copy.start()
    for copy in copies:
        copy.wait()


def finish(*arrays):
    vmem = pl.BlockSpec(memory_space=pltpu.VMEM)
    anywhere = pl.BlockSpec(memory_space=pl.ANY)
    return pl.pallas_call(
        finish_kernel,
        out_shape=tuple(jax.ShapeDtypeStruct(a.shape, a.dtype) for a in arrays),
        in_specs=[vmem] * 3,
        out_specs=(anywhere,) * 3,
        scratch_shapes=[pltpu.SemaphoreType.DMA((3,))],
        compiler_params=pltpu.CompilerParams(vmem_limit_bytes=4 * 2**20),
        name="finish",
    )(*arrays)


def shards(act, og, left_state, right_state, left_root_old, right_root_old, refresh):
    update, left_new, right_new = finish(
        *step(
            refresh,
            act,
            og,
            left_state[0, 0],
            right_state[0, 0],
            left_root_old[0, 0],
            right_root_old[0, 0],
        )
    )
    return update[:, None], left_new[None, None], right_new[None, None]


def solution(mesh):
    placed = (
        P("dp", ("mp", "helper")),
        P("dp", None),
        P("mp", "dp", "helper", None),
        P("mp", "dp", "helper", None),
        P("mp", "dp", "helper", None),
        P("mp", "dp", None, None),
        P("mp", "dp"),
    )
    return jax.shard_map(
        shards,
        mesh=mesh,
        in_specs=placed,
        out_specs=(
            P(None, "helper", None, "dp"),
            P("mp", "dp", "helper", None),
            P("mp", "dp", "helper", None),
        ),
        check_vma=False,
    )
```

```python
import jax
import jax.numpy as jnp
from jax import lax
from jax.experimental import pallas as pl
from jax.experimental.pallas import tpu as pltpu
from jax.sharding import PartitionSpec as P

decay_rate = 0.95
epsilon = 1e-06

NZ, NX, NY = 8, 4, 4
BLK = 512
PIECE = 256
TOKENS = 128
ROWS = 32
ORDER = (0, 1, 7, 2, 6, 3, 5, 4)
SLOT = {distance: slot for slot, distance in enumerate(ORDER)}
STAGES = ((0, 0, 8), (1, 0, 8), (2, 0, 8), (3, 0, 4), (3, 4, 8))
VMEM_LIMIT = 56 * 2**20
MESH = pl.DeviceIdType.MESH


def place():
    d = lax.axis_index("dp")
    return d // NX, d % NX, lax.axis_index("mp"), lax.axis_index("helper")


def remote(src, dst, send, recv, device):
    return pltpu.make_async_remote_copy(
        src_ref=src,
        dst_ref=dst,
        send_sem=send,
        recv_sem=recv,
        device_id=device,
        device_id_type=MESH,
    )


def across_rows(a, b):
    return lax.dot_general(a, b, (((0,), (0,)), ((), ())), preferred_element_type=jnp.float32)


def inverse_root(s):
    b16 = jnp.bfloat16
    scale = BLK * jnp.sqrt(jnp.sum(s * s) * (1.0 / (BLK * BLK)) + epsilon)
    first = s * (1.0 / scale)
    first16 = first.astype(b16)
    second = jnp.dot(first16, first16, preferred_element_type=jnp.float32)
    third = jnp.dot(second.astype(b16), first16, preferred_element_type=jnp.float32)
    upper = (250.0 / 4096) * first - (25.0 / 4096) * second + (1.0 / 4096) * third
    high = jnp.dot(third.astype(b16), upper.astype(b16), preferred_element_type=jnp.float32)
    rows = lax.broadcasted_iota(jnp.int32, s.shape, 0)
    columns = lax.broadcasted_iota(jnp.int32, s.shape, 1)
    constant = jnp.where(rows == columns, 25.0 / 16, 0.0)
    low = (-5.0 / 16 - 3125.0 / 4096) * first + (3125.0 / 4096) * second - (1250.0 / 4096) * third
    return ((constant + low + high) * lax.rsqrt(jnp.sqrt(scale))).astype(b16)


def step_kernel(
    fresh,
    act_ref,
    og_ref,
    left_ref,
    right_ref,
    lroot_ref,
    rroot_ref,
    out,
    left_new,
    right_new,
    act_buf,
    act_t,
    og_buf,
    part_out,
    part_in,
    grad_buf,
    stats,
    lroot,
    rroot,
    piece,
    shaped,
    total,
    own_sem,
    z_send,
    z_recv,
    a_send,
    a_recv,
    x_send,
    x_recv,
    y_send,
    y_recv,
    r_send,
    r_recv,
    s_send,
    s_recv,
    u_send,
    u_recv,
    out_sem,
):
    z, x, y, h = place()

    pair = x + 1 - 2 * lax.rem(x, 2)
    partner = NX - 1 - x

    def at(dz, column=x):
        return (lax.rem(z + dz, NZ) * NX + column, y, h)

    def crossed(dz, column=x):
        return (lax.rem(z + dz, NZ) * NX + column, y, 1 - h)

    def at_y(k):
        return (z * NX + x, lax.rem(y + k, NY), h)

    sibling = crossed(0)
    barrier = pltpu.get_barrier_semaphore()
    peers = [crossed(dz) for dz in range(NZ)] + [crossed(dz, pair) for dz in range(NZ)]
    peers += [at(1), at(7), at(0, pair), at(0, partner), at_y(1), at_y(3)]
    for peer in peers:
        pl.semaphore_signal(barrier, inc=1, device_id=peer, device_id_type=MESH)

    def start(copies):
        for copy in copies:
            copy.start()

    def await_bytes(ref, sem):
        pltpu.make_async_copy(ref, ref, sem).wait()

    here = pl.ds(pl.multiple_of(h * PIECE, PIECE), PIECE)

    def target(c):
        owner = pair if c % 2 else x
        return owner, (owner if c >= 2 else NX - 1 - owner)

    def og_part(dz, c):
        column = (lax.rem(z + dz, NZ) * NX + target(c)[1]) * BLK
        return og_ref.at[
            pl.ds(pl.multiple_of(y * ROWS, ROWS), ROWS), pl.ds(pl.multiple_of(column, BLK), BLK)
        ]

    left_in = pltpu.make_async_copy(left_ref, stats.at[0, here], own_sem.at[2])
    right_in = pltpu.make_async_copy(right_ref, stats.at[1, here], own_sem.at[3])
    lroot_in = pltpu.make_async_copy(lroot_ref, lroot.at[here], own_sem.at[4])
    rroot_in = pltpu.make_async_copy(rroot_ref, rroot, own_sem.at[5])
    left_over = remote(left_ref, stats.at[0, here], s_send.at[0], s_recv.at[0], sibling)
    right_over = remote(right_ref, stats.at[1, here], s_send.at[1], s_recv.at[1], sibling)
    lroot_over = remote(lroot_ref, lroot.at[here], s_send.at[2], s_recv.at[2], sibling)
    rroot_over = remote(rroot, rroot, s_send.at[4], s_recv.at[4], sibling)

    def renew_left(grad):
        stats[0] = stats[0] + lax.dot_general(
            grad, grad, (((1,), (1,)), ((), ())), preferred_element_type=jnp.float32
        )
        lroot[...] = jnp.where(fresh[0, 0] > 0, inverse_root(stats[0]), lroot[...])

    g_copy = remote(grad_buf, grad_buf, s_send.at[3], s_recv.at[3], sibling)
    pl.semaphore_wait(barrier, len(peers))

    @pl.when(h == 0)
    def _():
        start(
            [
                remote(act_ref, act_buf.at[0, SLOT[1], 0], a_send, a_recv.at[0], crossed(1)),
                remote(act_ref, act_buf.at[0, SLOT[7], 0], a_send, a_recv.at[0], crossed(7)),
                remote(act_ref, act_buf.at[0, 0, 0], a_send, a_recv.at[4], sibling),
            ]
        )
        for i, (c, first, end) in enumerate(STAGES):
            for slot in reversed(range(first, end)):
                if slot or c % 2:
                    remote(
                        og_part(ORDER[slot], c),
                        og_buf.at[c, slot, y],
                        z_send,
                        z_recv.at[i],
                        crossed(ORDER[slot], target(c)[0]),
                    ).start()
            if i == 0:
                remote(act_ref, act_buf.at[1, 0, 0], a_send, x_recv, crossed(0, pair)).start()
        start([left_in, right_in, lroot_in, left_over, right_over, lroot_over])
        for copy in (left_in, right_in, lroot_in, left_over, lroot_over):
            copy.wait()
        stats[0] = decay_rate * stats[0]
        stats[1, here] = decay_rate * stats[1, here]
        g_copy.wait_recv()
        renew_left(grad_buf[...])
        rroot_over.wait_recv()

    @pl.when(h == 1)
    def _():
        own_og = [
            pltpu.make_async_copy(og_part(0, c), og_buf.at[c, 0, y], own_sem.at[c * 3])
            for c in (0, 2)
        ]
        own_act = pltpu.make_async_copy(act_ref, act_buf.at[0, 0, 1], own_sem.at[1])

        def send_act(i):
            up, down = act_buf.at[0, SLOT[i]], act_buf.at[0, SLOT[-i % NZ]]
            if i < 4:
                to_up, to_down = act_buf.at[0, SLOT[i + 1]], act_buf.at[0, SLOT[7 - i]]
                if i == 3:
                    up, to_up, down, to_down = up.at[0], to_up.at[0], down.at[1], to_down.at[1]
                if i == 0:
                    up, to_up, down, to_down = act_ref, to_up.at[1], act_ref, to_down.at[1]
                start(
                    [
                        remote(up, to_up, a_send, a_recv.at[i], at(1)),
                        remote(down, to_down, a_send, a_recv.at[i], at(7)),
                    ]
                )
            if i == 0:
                remote(act_ref, act_buf.at[1, 0, 1], x_send, x_recv, at(0, pair)).start()
                return
            for slot in (SLOT[i], SLOT[-i % NZ]) if i < 4 else (SLOT[i],):
                src, dst = act_buf.at[0, slot], act_buf.at[1, slot]
                remote(src, dst, x_send, x_recv, at(0, pair)).start()

        def next_act(i):
            await_bytes(act_buf.at[0, 0:2] if i < 4 else act_buf.at[0, 0], a_recv.at[i - 1])
            send_act(i)

        low, high = lax.rem(y + 3, NY), lax.rem(y + 1, NY)

        def first_y(i):
            c, first, end = STAGES[i]
            if c % 2 == 0:
                own_og[c // 2].wait()
            await_bytes(og_buf.at[c, first if c % 2 else first + 1 : end, 0], z_recv.at[i])
            mine = og_buf.at[c, first:end, y]
            start(
                [
                    remote(mine, mine, y_send, y_recv.at[i, 0], at_y(1)),
                    remote(mine, mine, y_send, y_recv.at[i, 0], at_y(3)),
                ]
            )

        def second_y(i):
            c, first, end = STAGES[i]
            await_bytes(og_buf.at[c, first:end, 0:2], y_recv.at[i, 0])
            middle = (first + end) // 2
            up, down = og_buf.at[c, first:middle, low], og_buf.at[c, middle:end, high]
            start(
                [
                    remote(up, up, y_send, y_recv.at[i, 1], at_y(1)),
                    remote(down, down, y_send, y_recv.at[i, 1], at_y(3)),
                ]
            )

        def turn(bank):
            for half in range(2):
                columns = act_buf[bank, :, half].reshape(NZ * TOKENS, PIECE)
                act_t[bank, pl.ds(half * PIECE, PIECE)] = columns.T

        def product(i):
            c, first, end = STAGES[i]
            await_bytes(og_buf.at[c, first:end, 0], y_recv.at[i, 1])
            rows = og_buf[c, first:end].reshape((end - first) * TOKENS, BLK)
            columns = act_t[c % 2, :, first * TOKENS : end * TOKENS]
            return jnp.dot(columns, rows, preferred_element_type=jnp.float32)

        start(own_og + [own_act])
        send_act(0)
        next_act(1)
        first_y(0)
        next_act(2)
        start([left_in, right_in, lroot_in, rroot_in, left_over, lroot_over])
        first_y(1)
        second_y(0)
        next_act(3)
        first_y(2)
        second_y(1)
        own_act.wait()
        await_bytes(act_buf.at[0, 0, 0], a_recv.at[4])
        next_act(4)
        turn(0)
        total[...] = product(0)
        first_y(3)
        second_y(2)
        await_bytes(act_buf.at[1], x_recv)
        turn(1)
        part_out[...] = (total[...] + product(1)).astype(jnp.bfloat16)
        r_copy = remote(part_out, part_in, r_send, r_recv, at(0, partner))
        r_copy.start()
        first_y(4)
        second_y(3)
        total[...] = product(2)
        second_y(4)
        total[...] = total[...] + product(3)
        for copy in (left_in, right_in, lroot_in, rroot_in, left_over, lroot_over):
            copy.wait()
        right_over.wait_recv()
        stats[...] = decay_rate * stats[...]
        r_copy.wait_recv()
        total[...] = total[...] + part_in[...].astype(jnp.float32)
        grad_buf[...] = (total[...] + product(4)).astype(jnp.bfloat16)
        g_copy.start()
        grad = grad_buf[...]
        stats[1] = stats[1] + across_rows(grad, grad)
        rroot[...] = jnp.where(fresh[0, 0] > 0, inverse_root(stats[1]), rroot[...])
        rroot_over.start()
        renew_left(grad)

    grad = grad_buf[...]
    grad_wide = grad.astype(jnp.float32)
    grad_square = jnp.sum(grad_wide * grad_wide)
    right_copy = pltpu.make_async_copy(stats.at[1, here], right_new, out_sem.at[0])
    left_copy = pltpu.make_async_copy(stats.at[0, here], left_new, out_sem.at[1])
    left_copy.start()
    half = jnp.dot(lroot[...], grad, preferred_element_type=jnp.float32).astype(jnp.bfloat16)
    shaped[...] = jnp.dot(half, rroot[...], preferred_element_type=jnp.float32)
    entries = 1.0 / (BLK * BLK)
    ratio = jnp.sqrt(grad_square * entries + epsilon) / jnp.sqrt(
        jnp.sum(shaped[...] * shaped[...]) * entries + epsilon
    )
    piece[...] = (ratio * shaped[here]).astype(jnp.bfloat16)

    below, above = lax.rem(y + 3, NY), lax.rem(y + 1, NY)
    bottom, top = pl.ds(0, PIECE // 2), pl.ds(PIECE // 2, PIECE // 2)

    def spread(i, rows, owner, k):
        src = piece.at[rows] if owner is y else out.at[owner, rows]
        return remote(src, out.at[owner, rows], u_send.at[i], u_recv.at[i], at_y(k))

    first = [spread(0, bottom, y, 1), spread(1, top, y, 3)]
    rest = [spread(2, top, y, 1), spread(3, bottom, y, 3)]
    second = [spread(4, bottom, below, 1), spread(5, top, above, 3)]
    start(first + rest)
    own_copy = pltpu.make_async_copy(piece, out.at[y], out_sem.at[2])
    own_copy.start()

    @pl.when(h == 0)
    def _():
        stats[1, here] = stats[1, here] + across_rows(grad_buf[:, 0:PIECE], grad_buf[...])
        right_copy.start()
        right_over.wait_send()
        await_bytes(act_buf.at[0, 0:2], a_send)
        await_bytes(og_buf.at[0:3, 0:5, 0:2], z_send)

    @pl.when(h == 1)
    def _():
        right_copy.start()
        rroot_over.wait_send()
        await_bytes(act_buf.at[0, 0:6], a_send)
        await_bytes(og_buf.at[0:3, 0:5, 0:2], x_send)
        await_bytes(og_buf.at[:, :, 0:3], y_send)
        await_bytes(part_out, r_send)
        g_copy.wait_send()

    for one, two in zip(first, second):
        one.wait_recv()
        two.start()
    for copy in rest + second:
        copy.wait_recv()
    for copy in first + rest + second:
        copy.wait_send()
    for copy in (right_copy, left_copy, own_copy):
        copy.wait()


def step(fresh, act, og, left, right, lroot, rroot):
    hbm = pl.BlockSpec(memory_space=pl.ANY)
    dma = pltpu.SemaphoreType.DMA
    f32, b16 = jnp.float32, jnp.bfloat16
    return pl.pallas_call(
        step_kernel,
        out_shape=(
            pltpu.VMEM((NY, PIECE, BLK), b16),
            pltpu.VMEM((PIECE, BLK), f32),
            pltpu.VMEM((PIECE, BLK), f32),
        ),
        in_specs=[pl.BlockSpec(memory_space=pltpu.SMEM)] + [hbm] * 6,
        out_specs=(hbm,) * 3,
        scratch_shapes=[
            pltpu.VMEM((2, NZ, 2, TOKENS, PIECE), b16),
            pltpu.VMEM((2, BLK, NZ * TOKENS), b16),
            pltpu.VMEM((4, NZ, NY, ROWS, BLK), b16),
            pltpu.VMEM((BLK, BLK), b16),
            pltpu.VMEM((BLK, BLK), b16),
            pltpu.VMEM((BLK, BLK), b16),
            pltpu.VMEM((2, BLK, BLK), f32),
            pltpu.VMEM((BLK, BLK), b16),
            pltpu.VMEM((BLK, BLK), b16),
            pltpu.VMEM((PIECE, BLK), b16),
            pltpu.VMEM((BLK, BLK), f32),
            pltpu.VMEM((BLK, BLK), f32),
            dma((7,)),
            dma,
            dma((5,)),
            dma,
            dma((5,)),
            dma,
            dma,
            dma,
            dma((5, 2)),
            dma,
            dma,
            dma((5,)),
            dma((5,)),
            dma((6,)),
            dma((6,)),
            dma((3,)),
        ],
        compiler_params=pltpu.CompilerParams(
            collective_id=0, has_side_effects=True, vmem_limit_bytes=VMEM_LIMIT
        ),
        name="step",
    )(fresh, act, og, left, right, lroot, rroot)


def finish_kernel(update, left, right, update_out, left_out, right_out, sems):
    copies = [
        pltpu.make_async_copy(update, update_out, sems.at[0]),
        pltpu.make_async_copy(left, left_out, sems.at[1]),
        pltpu.make_async_copy(right, right_out, sems.at[2]),
    ]
    for copy in copies:
        copy.start()
    for copy in copies:
        copy.wait()


def finish(*arrays):
    vmem = pl.BlockSpec(memory_space=pltpu.VMEM)
    anywhere = pl.BlockSpec(memory_space=pl.ANY)
    return pl.pallas_call(
        finish_kernel,
        out_shape=tuple(jax.ShapeDtypeStruct(a.shape, a.dtype) for a in arrays),
        in_specs=[vmem] * 3,
        out_specs=(anywhere,) * 3,
        scratch_shapes=[pltpu.SemaphoreType.DMA((3,))],
        compiler_params=pltpu.CompilerParams(vmem_limit_bytes=4 * 2**20),
        name="finish",
    )(*arrays)


def shards(act, og, left_state, right_state, left_root_old, right_root_old, refresh):
    update, left_new, right_new = finish(
        *step(
            refresh,
            act,
            og,
            left_state[0, 0],
            right_state[0, 0],
            left_root_old[0, 0],
            right_root_old[0, 0],
        )
    )
    return update[:, None], left_new[None, None], right_new[None, None]


def solution(mesh):
    placed = (
        P("dp", ("mp", "helper")),
        P("dp", None),
        P("mp", "dp", "helper", None),
        P("mp", "dp", "helper", None),
        P("mp", "dp", "helper", None),
        P("mp", "dp", None, None),
        P("mp", "dp"),
    )
    return jax.shard_map(
        shards,
        mesh=mesh,
        in_specs=placed,
        out_specs=(
            P(None, "helper", None, "dp"),
            P("mp", "dp", "helper", None),
            P("mp", "dp", "helper", None),
        ),
        check_vma=False,
    )
```

```python
import jax
import jax.numpy as jnp
from jax import lax
from jax.experimental import pallas as pl
from jax.experimental.pallas import tpu as pltpu
from jax.sharding import PartitionSpec as P

decay_rate = 0.95
epsilon = 1e-06

NZ, NX, NY = 8, 4, 4
BLK = 512
PIECE = 256
TOKENS = 128
ROWS = 32
ORDER = (0, 1, 7, 2, 6, 3, 5, 4)
SLOT = {distance: slot for slot, distance in enumerate(ORDER)}
STAGES = ((0, 0, 8), (1, 0, 8), (2, 0, 8), (3, 0, 4), (3, 4, 8))
VMEM_LIMIT = 56 * 2**20
MESH = pl.DeviceIdType.MESH


def place():
    d = lax.axis_index("dp")
    return d // NX, d % NX, lax.axis_index("mp"), lax.axis_index("helper")


def remote(src, dst, send, recv, device):
    return pltpu.make_async_remote_copy(
        src_ref=src,
        dst_ref=dst,
        send_sem=send,
        recv_sem=recv,
        device_id=device,
        device_id_type=MESH,
    )


def across_rows(a, b):
    return lax.dot_general(a, b, (((0,), (0,)), ((), ())), preferred_element_type=jnp.float32)


def inverse_root(s):
    b16 = jnp.bfloat16
    scale = BLK * jnp.sqrt(jnp.sum(s * s) * (1.0 / (BLK * BLK)) + epsilon)
    first = s * (1.0 / scale)
    first16 = first.astype(b16)
    second = jnp.dot(first16, first16, preferred_element_type=jnp.float32)
    third = jnp.dot(second.astype(b16), first16, preferred_element_type=jnp.float32)
    upper = (250.0 / 4096) * first - (25.0 / 4096) * second + (1.0 / 4096) * third
    high = jnp.dot(third.astype(b16), upper.astype(b16), preferred_element_type=jnp.float32)
    rows = lax.broadcasted_iota(jnp.int32, s.shape, 0)
    columns = lax.broadcasted_iota(jnp.int32, s.shape, 1)
    constant = jnp.where(rows == columns, 25.0 / 16, 0.0)
    low = (-5.0 / 16 - 3125.0 / 4096) * first + (3125.0 / 4096) * second - (1250.0 / 4096) * third
    return ((constant + low + high) * lax.rsqrt(jnp.sqrt(scale))).astype(b16)


def step_kernel(
    fresh,
    act_ref,
    og_ref,
    left_ref,
    right_ref,
    lroot_ref,
    rroot_ref,
    out,
    left_new,
    right_new,
    act_buf,
    act_t,
    og_buf,
    part_out,
    part_in,
    grad_buf,
    stats,
    lroot,
    rroot,
    piece,
    shaped,
    total,
    own_sem,
    z_send,
    z_recv,
    a_send,
    a_recv,
    x_send,
    x_recv,
    y_send,
    y_recv,
    r_send,
    r_recv,
    s_send,
    s_recv,
    u_send,
    u_recv,
    out_sem,
):
    z, x, y, h = place()

    pair = x + 1 - 2 * lax.rem(x, 2)
    partner = NX - 1 - x

    def at(dz, column=x):
        return (lax.rem(z + dz, NZ) * NX + column, y, h)

    def crossed(dz, column=x):
        return (lax.rem(z + dz, NZ) * NX + column, y, 1 - h)

    def at_y(k):
        return (z * NX + x, lax.rem(y + k, NY), h)

    sibling = crossed(0)
    barrier = pltpu.get_barrier_semaphore()
    peers = [crossed(dz) for dz in range(NZ)] + [crossed(dz, pair) for dz in range(NZ)]
    peers += [at(1), at(7), at(0, pair), at(0, partner), at_y(1), at_y(3)]
    for peer in peers:
        pl.semaphore_signal(barrier, inc=1, device_id=peer, device_id_type=MESH)

    def start(copies):
        for copy in copies:
            copy.start()

    def await_bytes(ref, sem):
        pltpu.make_async_copy(ref, ref, sem).wait()

    here = pl.ds(pl.multiple_of(h * PIECE, PIECE), PIECE)

    def target(c):
        owner = pair if c % 2 else x
        return owner, (owner if c >= 2 else NX - 1 - owner)

    def og_part(dz, c):
        column = (lax.rem(z + dz, NZ) * NX + target(c)[1]) * BLK
        return og_ref.at[
            pl.ds(pl.multiple_of(y * ROWS, ROWS), ROWS), pl.ds(pl.multiple_of(column, BLK), BLK)
        ]

    def old_copies():
        return [
            pltpu.make_async_copy(left_ref, stats.at[0, here], own_sem.at[2]),
            pltpu.make_async_copy(right_ref, stats.at[1, here], own_sem.at[3]),
            pltpu.make_async_copy(lroot_ref, lroot.at[here], own_sem.at[4]),
            pltpu.make_async_copy(rroot_ref, rroot, own_sem.at[5]),
            remote(left_ref, stats.at[0, here], s_send.at[0], s_recv.at[0], sibling),
            remote(right_ref, stats.at[1, here], s_send.at[1], s_recv.at[1], sibling),
            remote(lroot_ref, lroot.at[here], s_send.at[2], s_recv.at[2], sibling),
        ]

    def age():
        for copy in old_copies():
            copy.wait()

    g_copy = remote(grad_buf, grad_buf, s_send.at[3], s_recv.at[3], sibling)
    pl.semaphore_wait(barrier, len(peers))

    @pl.when(h == 0)
    def _():
        start(
            [
                remote(act_ref, act_buf.at[0, SLOT[1], 0], a_send, a_recv.at[0], crossed(1)),
                remote(act_ref, act_buf.at[0, SLOT[7], 0], a_send, a_recv.at[0], crossed(7)),
                remote(act_ref, act_buf.at[0, 0, 0], a_send, a_recv.at[4], sibling),
            ]
        )
        for i, (c, first, end) in enumerate(STAGES):
            for slot in reversed(range(first, end)):
                if slot or c % 2:
                    remote(
                        og_part(ORDER[slot], c),
                        og_buf.at[c, slot, y],
                        z_send,
                        z_recv.at[i],
                        crossed(ORDER[slot], target(c)[0]),
                    ).start()
            if i == 0:
                remote(act_ref, act_buf.at[1, 0, 0], a_send, x_recv, crossed(0, pair)).start()
        start(old_copies())
        age()
        g_copy.wait_recv()

    @pl.when(h == 1)
    def _():
        own_og = [
            pltpu.make_async_copy(og_part(0, c), og_buf.at[c, 0, y], own_sem.at[c * 3])
            for c in (0, 2)
        ]
        own_act = pltpu.make_async_copy(act_ref, act_buf.at[0, 0, 1], own_sem.at[1])

        def send_act(i):
            up, down = act_buf.at[0, SLOT[i]], act_buf.at[0, SLOT[-i % NZ]]
            if i < 4:
                to_up, to_down = act_buf.at[0, SLOT[i + 1]], act_buf.at[0, SLOT[7 - i]]
                if i == 3:
                    up, to_up, down, to_down = up.at[0], to_up.at[0], down.at[1], to_down.at[1]
                if i == 0:
                    up, to_up, down, to_down = act_ref, to_up.at[1], act_ref, to_down.at[1]
                start(
                    [
                        remote(up, to_up, a_send, a_recv.at[i], at(1)),
                        remote(down, to_down, a_send, a_recv.at[i], at(7)),
                    ]
                )
            if i == 0:
                remote(act_ref, act_buf.at[1, 0, 1], x_send, x_recv, at(0, pair)).start()
                return
            for slot in (SLOT[i], SLOT[-i % NZ]) if i < 4 else (SLOT[i],):
                src, dst = act_buf.at[0, slot], act_buf.at[1, slot]
                remote(src, dst, x_send, x_recv, at(0, pair)).start()

        def next_act(i):
            await_bytes(act_buf.at[0, 0:2] if i < 4 else act_buf.at[0, 0], a_recv.at[i - 1])
            send_act(i)

        low, high = lax.rem(y + 3, NY), lax.rem(y + 1, NY)

        def first_y(i):
            c, first, end = STAGES[i]
            if c % 2 == 0:
                own_og[c // 2].wait()
            await_bytes(og_buf.at[c, first if c % 2 else first + 1 : end, 0], z_recv.at[i])
            mine = og_buf.at[c, first:end, y]
            start(
                [
                    remote(mine, mine, y_send, y_recv.at[i, 0], at_y(1)),
                    remote(mine, mine, y_send, y_recv.at[i, 0], at_y(3)),
                ]
            )

        def second_y(i):
            c, first, end = STAGES[i]
            await_bytes(og_buf.at[c, first:end, 0:2], y_recv.at[i, 0])
            middle = (first + end) // 2
            up, down = og_buf.at[c, first:middle, low], og_buf.at[c, middle:end, high]
            start(
                [
                    remote(up, up, y_send, y_recv.at[i, 1], at_y(1)),
                    remote(down, down, y_send, y_recv.at[i, 1], at_y(3)),
                ]
            )

        def turn(bank):
            for half in range(2):
                columns = act_buf[bank, :, half].reshape(NZ * TOKENS, PIECE)
                act_t[bank, pl.ds(half * PIECE, PIECE)] = columns.T

        def product(i):
            c, first, end = STAGES[i]
            await_bytes(og_buf.at[c, first:end, 0], y_recv.at[i, 1])
            rows = og_buf[c, first:end].reshape((end - first) * TOKENS, BLK)
            columns = act_t[c % 2, :, first * TOKENS : end * TOKENS]
            return jnp.dot(columns, rows, preferred_element_type=jnp.float32)

        start(own_og + [own_act])
        send_act(0)
        next_act(1)
        first_y(0)
        next_act(2)
        start(old_copies())
        first_y(1)
        second_y(0)
        next_act(3)
        first_y(2)
        second_y(1)
        own_act.wait()
        await_bytes(act_buf.at[0, 0, 0], a_recv.at[4])
        next_act(4)
        turn(0)
        total[...] = product(0)
        first_y(3)
        second_y(2)
        await_bytes(act_buf.at[1], x_recv)
        turn(1)
        part_out[...] = (total[...] + product(1)).astype(jnp.bfloat16)
        r_copy = remote(part_out, part_in, r_send, r_recv, at(0, partner))
        r_copy.start()
        first_y(4)
        second_y(3)
        total[...] = product(2)
        second_y(4)
        total[...] = total[...] + product(3)
        age()
        r_copy.wait_recv()
        total[...] = total[...] + part_in[...].astype(jnp.float32)
        grad_buf[...] = (total[...] + product(4)).astype(jnp.bfloat16)
        g_copy.start()

    grad = grad_buf[...]
    grad_wide = grad.astype(jnp.float32)
    grad_square = jnp.sum(grad_wide * grad_wide)
    stats[1] = decay_rate * stats[1] + across_rows(grad, grad)
    right_copy = pltpu.make_async_copy(stats.at[1, here], right_new, out_sem.at[0])
    right_copy.start()
    stats[0] = decay_rate * stats[0] + lax.dot_general(
        grad, grad, (((1,), (1,)), ((), ())), preferred_element_type=jnp.float32
    )
    left_copy = pltpu.make_async_copy(stats.at[0, here], left_new, out_sem.at[1])
    left_copy.start()
    renew = fresh[0, 0] > 0
    lroot[...] = jnp.where(renew, inverse_root(stats[0]), lroot[...])
    rroot[...] = jnp.where(renew, inverse_root(stats[1]), rroot[...])
    half = jnp.dot(lroot[...], grad, preferred_element_type=jnp.float32).astype(jnp.bfloat16)
    shaped[...] = jnp.dot(half, rroot[...], preferred_element_type=jnp.float32)
    entries = 1.0 / (BLK * BLK)
    ratio = jnp.sqrt(grad_square * entries + epsilon) / jnp.sqrt(
        jnp.sum(shaped[...] * shaped[...]) * entries + epsilon
    )
    piece[...] = (ratio * shaped[here]).astype(jnp.bfloat16)

    below, above = lax.rem(y + 3, NY), lax.rem(y + 1, NY)
    bottom, top = pl.ds(0, PIECE // 2), pl.ds(PIECE // 2, PIECE // 2)

    def spread(i, rows, owner, k):
        src = piece.at[rows] if owner is y else out.at[owner, rows]
        return remote(src, out.at[owner, rows], u_send.at[i], u_recv.at[i], at_y(k))

    first = [spread(0, bottom, y, 1), spread(1, top, y, 3)]
    rest = [spread(2, top, y, 1), spread(3, bottom, y, 3)]
    second = [spread(4, bottom, below, 1), spread(5, top, above, 3)]
    start(first + rest)
    own_copy = pltpu.make_async_copy(piece, out.at[y], out_sem.at[2])
    own_copy.start()

    @pl.when(h == 0)
    def _():
        await_bytes(act_buf.at[0, 0:2], a_send)
        await_bytes(og_buf.at[0:3, 0:5, 0:2], z_send)

    @pl.when(h == 1)
    def _():
        await_bytes(act_buf.at[0, 0:6], a_send)
        await_bytes(og_buf.at[0:3, 0:5, 0:2], x_send)
        await_bytes(og_buf.at[:, :, 0:3], y_send)
        await_bytes(part_out, r_send)
        g_copy.wait_send()

    for one, two in zip(first, second):
        one.wait_recv()
        two.start()
    for copy in rest + second:
        copy.wait_recv()
    for copy in first + rest + second:
        copy.wait_send()
    for copy in (right_copy, left_copy, own_copy):
        copy.wait()


def step(fresh, act, og, left, right, lroot, rroot):
    hbm = pl.BlockSpec(memory_space=pl.ANY)
    dma = pltpu.SemaphoreType.DMA
    f32, b16 = jnp.float32, jnp.bfloat16
    return pl.pallas_call(
        step_kernel,
        out_shape=(
            pltpu.VMEM((NY, PIECE, BLK), b16),
            pltpu.VMEM((PIECE, BLK), f32),
            pltpu.VMEM((PIECE, BLK), f32),
        ),
        in_specs=[pl.BlockSpec(memory_space=pltpu.SMEM)] + [hbm] * 6,
        out_specs=(hbm,) * 3,
        scratch_shapes=[
            pltpu.VMEM((2, NZ, 2, TOKENS, PIECE), b16),
            pltpu.VMEM((2, BLK, NZ * TOKENS), b16),
            pltpu.VMEM((4, NZ, NY, ROWS, BLK), b16),
            pltpu.VMEM((BLK, BLK), b16),
            pltpu.VMEM((BLK, BLK), b16),
            pltpu.VMEM((BLK, BLK), b16),
            pltpu.VMEM((2, BLK, BLK), f32),
            pltpu.VMEM((BLK, BLK), b16),
            pltpu.VMEM((BLK, BLK), b16),
            pltpu.VMEM((PIECE, BLK), b16),
            pltpu.VMEM((BLK, BLK), f32),
            pltpu.VMEM((BLK, BLK), f32),
            dma((7,)),
            dma,
            dma((5,)),
            dma,
            dma((5,)),
            dma,
            dma,
            dma,
            dma((5, 2)),
            dma,
            dma,
            dma((4,)),
            dma((4,)),
            dma((6,)),
            dma((6,)),
            dma((3,)),
        ],
        compiler_params=pltpu.CompilerParams(
            collective_id=0, has_side_effects=True, vmem_limit_bytes=VMEM_LIMIT
        ),
        name="step",
    )(fresh, act, og, left, right, lroot, rroot)


def finish_kernel(update, left, right, update_out, left_out, right_out, sems):
    copies = [
        pltpu.make_async_copy(update, update_out, sems.at[0]),
        pltpu.make_async_copy(left, left_out, sems.at[1]),
        pltpu.make_async_copy(right, right_out, sems.at[2]),
    ]
    for copy in copies:
        copy.start()
    for copy in copies:
        copy.wait()


def finish(*arrays):
    vmem = pl.BlockSpec(memory_space=pltpu.VMEM)
    anywhere = pl.BlockSpec(memory_space=pl.ANY)
    return pl.pallas_call(
        finish_kernel,
        out_shape=tuple(jax.ShapeDtypeStruct(a.shape, a.dtype) for a in arrays),
        in_specs=[vmem] * 3,
        out_specs=(anywhere,) * 3,
        scratch_shapes=[pltpu.SemaphoreType.DMA((3,))],
        compiler_params=pltpu.CompilerParams(vmem_limit_bytes=4 * 2**20),
        name="finish",
    )(*arrays)


def shards(act, og, left_state, right_state, left_root_old, right_root_old, refresh):
    update, left_new, right_new = finish(
        *step(
            refresh,
            act,
            og,
            left_state[0, 0],
            right_state[0, 0],
            left_root_old[0, 0],
            right_root_old[0, 0],
        )
    )
    return update[:, None], left_new[None, None], right_new[None, None]


def solution(mesh):
    placed = (
        P("dp", ("mp", "helper")),
        P("dp", None),
        P("mp", "dp", "helper", None),
        P("mp", "dp", "helper", None),
        P("mp", "dp", "helper", None),
        P("mp", "dp", None, None),
        P("mp", "dp"),
    )
    return jax.shard_map(
        shards,
        mesh=mesh,
        in_specs=placed,
        out_specs=(
            P(None, "helper", None, "dp"),
            P("mp", "dp", "helper", None),
            P("mp", "dp", "helper", None),
        ),
        check_vma=False,
    )
```
